32 devices in a mesh: gx: 8 (over z, y), gy: 4 (over x, core).
Axes of the slice: x: 2, y: 2, z: 4, core: 2. Of those that a mesh axis runs over, the one named last changes fastest.
Arguments:
- vectors: float32 [8, 3, 4, 64, 512], P(None, None, None, 'gx', 'gy'), may hold values from -2000 to 2000, as said below
- background: float32 [3, 4, 64, 512], P(None, None, 'gx', 'gy'), may hold values from -1 to 1
- obs_site: int32 [131072], P(('gx', 'gy')), may hold values from 0 to 12287
- obs_offset: float32 [2, 131072], P(None, ('gx', 'gy')), may hold values from -1 to 1
- obs_error: float32 [131072], P(('gx', 'gy')), may hold values from 0.5 to 4
Outputs:
- analysis: float32 [8, 3, 4, 64, 512], P(None, None, None, 'gx', 'gy')
- obs_perturb: float32 [8, 131072], P(None, ('gx', 'gy'))
The draws below stay inside these ranges and needn't reach their ends.
Inputs may be any that keep to these rules, and one draw needn't show every extreme that they name: Drawn with scales that vary over vectors, variables, levels and cells. `obs_site`: observation n lies in the tile of device n // 4096; its site is ((variable * 4 + level) * 8 + row) * 128 + column, with row and column local to that tile.
All inputs are finite; a program needn't handle non-finite values.
Results may differ from the reference program's by a relative error of at most 0.000092.
Values sent between devices are 32-bit elements; how exact they have to be, the bound alone decides.
A program may use at most 192 MiB of HBM per device.

```python
import math
import jax
import jax.numpy as jnp
from jax import lax

K = 8
L = 4
CX = 8
CY = 128
OBS_DEV = 4096
NX = 64
NY = 512
NOBS = 131072
N_GY = 4


def draw_vectors(key, part):
    keys = jax.random.split(key, 4)
    cell_shape = (3, L, NX, NY)
    common = jnp.clip(jax.random.normal(keys[0], cell_shape, jnp.float32), -4.0, 4.0)
    own_part = jnp.clip(jax.random.normal(keys[1], (K,) + cell_shape, jnp.float32), -4.0, 4.0)
    common_weight = 0.6
    cell_range = 2.3
    field_scale = jnp.exp(jax.random.uniform(keys[2], (K, 3, L, 1, 1), jnp.float32, 0.0, 2.3))
    cell_scale = jnp.exp(jax.random.uniform(keys[3], (1, 1, 1, NX, NY), jnp.float32, 0.0, cell_range))
    ramp = (1.0 + 2.0 * jnp.arange(NX, dtype=jnp.float32) / NX).reshape(NX, 1)
    return (common_weight * common + own_part) * field_scale * cell_scale * ramp


def touch_ends(drawn, key, least, high):
    index_at = [jax.random.randint(jax.random.fold_in(key, axis), (), 0, length) for axis, length in enumerate(drawn.shape)]
    widest = drawn.shape.index(max(drawn.shape))
    next_to = index_at[:widest] + [(index_at[widest] + 1) % drawn.shape[widest]] + index_at[widest + 1:]
    return drawn.at[tuple(index_at)].set(least).at[tuple(next_to)].set(high)


def level_of(stream_key, extent, cuts, least, high):
    def one(position, blocks):
        steps = jax.random.uniform(jax.random.fold_in(jax.random.fold_in(stream_key, 6), position), (blocks,), jnp.float32, least / len(cuts), high / len(cuts))
        return jnp.repeat(jnp.exp(steps), extent[position] // blocks).reshape((-1,) + (1,) * (len(extent) - position - 1))

    factor_of = one(*cuts[0])
    for cut in cuts[1:]:
        factor_of = factor_of * one(*cut)
    return factor_of


def setup_inputs(seed: int = 0) -> dict:
    splits = jax.random.split(jax.random.key(seed), 6)
    vectors = draw_vectors(jax.random.fold_in(splits[5], 71), 0)
    background = jnp.clip(jax.random.uniform(splits[1], (3, L, NX, NY), jnp.float32, -1.0, 1.0) * level_of(splits[1], (3, L, NX, NY), ((2, 8), (3, 4)), -0.4, 0.0), -1.0, 1.0)
    obs_site = touch_ends(jax.random.randint(splits[2], (NOBS,), 0, 3 * L * CX * CY), jax.random.fold_in(splits[2], 1), 0, (3 * L * CX * CY) - 1).astype(jnp.int32)
    obs_offset = jnp.clip(jax.random.uniform(splits[3], (2, NOBS), jnp.float32, -1.0, 1.0) * level_of(splits[3], (2, NOBS), ((1, 32),), -0.4, 0.0), -1.0, 1.0)
    obs_error = jnp.clip(jnp.exp(math.log(4.0) - 2.0794415 * jax.random.uniform(splits[4], (NOBS,), jnp.float32) ** level_of(splits[4], (NOBS,), ((0, 32),), -0.2, 0.2)), 0.5, 4.0)
    return {"vectors": vectors, "background": background, "obs_site": obs_site, "obs_offset": obs_offset, "obs_error": obs_error}


step_size = 0.35
highest = lax.Precision.HIGHEST

def along_x(field):
    return 0.5 * (jnp.roll(field, -1, -2) - jnp.roll(field, 1, -2))

def along_y(field):
    return 0.5 * (jnp.roll(field, -1, -1) - jnp.roll(field, 1, -1))

def tendency(state, background):
    wind_x, wind_y, vort_abs = (background[0], background[1], background[2])
    east_part, north_part, height = (state[0], state[1], state[2])

    def advect(field):
        return wind_x * along_x(field) + wind_y * along_y(field)
    tend_east = -advect(east_part) - along_x(height) + vort_abs * north_part
    tend_north = -advect(north_part) - along_y(height) - vort_abs * east_part
    tend_height = -advect(height) - (along_x(east_part) + along_y(north_part))
    return jnp.stack([tend_east, tend_north, tend_height], axis=0)

def runge_kutta(state, background):
    section_one = state + step_size * tendency(state, background)
    section_two = 0.75 * state + 0.25 * (section_one + step_size * tendency(section_one, background))
    return state / 3.0 + 2.0 / 3.0 * (section_two + step_size * tendency(section_two, background))

def reference(vectors, background, obs_site, obs_offset, obs_error):
    bred = lax.map(lambda single: runge_kutta(single, background), vectors)
    flattened = bred.reshape(K, -1)
    cells_all = float(3 * L * NX * NY)
    gram = jnp.dot(flattened.astype(jnp.float32), flattened.T.astype(jnp.float32), precision=highest, preferred_element_type=jnp.float32) / cells_all
    count_index = jnp.arange(NOBS, dtype=jnp.int32)
    device = count_index // OBS_DEV
    plane_index = obs_site // (CX * CY)
    cell_index = obs_site % (CX * CY)
    row_index = device // N_GY * CX + cell_index // CY
    col_index = device % N_GY * CY + cell_index % CY
    shift_x = obs_offset[0]
    shift_y = obs_offset[1]
    weights_x = (jnp.maximum(-shift_x, 0.0), 1.0 - jnp.abs(shift_x), jnp.maximum(shift_x, 0.0))
    weights_y = (jnp.maximum(-shift_y, 0.0), 1.0 - jnp.abs(shift_y), jnp.maximum(shift_y, 0.0))
    projected = jnp.zeros((K, NOBS), jnp.float32)
    for step_x in (-1, 0, 1):
        for step_y in (-1, 0, 1):
            index = (plane_index * NX + (row_index + step_x) % NX) * NY + (col_index + step_y) % NY
            projected = projected + weights_x[step_x + 1] * weights_y[step_y + 1] * jnp.take(flattened, index.astype(jnp.int32), axis=1)
    normal = jnp.dot((projected / obs_error).astype(jnp.float32), projected.T.astype(jnp.float32), precision=highest, preferred_element_type=jnp.float32) / float(NOBS)
    identity = jnp.eye(K, dtype=jnp.float32)
    lower = jnp.linalg.cholesky(gram)
    inv_lower = lax.linalg.triangular_solve(lower, identity, left_side=True, lower=True)
    system = identity + jnp.dot(jnp.dot(inv_lower, normal, precision=highest), inv_lower.T, precision=highest)
    factor = jnp.linalg.cholesky(system)
    inv_factor = lax.linalg.triangular_solve(factor, identity, left_side=True, lower=True)
    combo = jnp.dot(inv_factor, inv_lower, precision=highest)
    analysis = jnp.dot(combo.astype(jnp.float32), flattened.astype(jnp.float32), precision=highest, preferred_element_type=jnp.float32).reshape(bred.shape)
    obs_perturb = jnp.dot(combo.astype(jnp.float32), projected.astype(jnp.float32), precision=highest, preferred_element_type=jnp.float32) / jnp.sqrt(obs_error)
    return (analysis, obs_perturb)
```

```python
import functools

import jax
import jax.numpy as jnp
from jax import lax
from jax.experimental import pallas as pl
from jax.experimental.pallas import tpu as pltpu
from jax.sharding import PartitionSpec as P

K = 8
V = 3
L = 4
ROWS = 8
COLS = 128
PLANES = V * L
STRIDE = PLANES * ROWS
STEP = 0.35
MESH = pl.DeviceIdType.MESH
SHIFTS = 5
N_EDGE = 8
N_COPIES = N_EDGE + 2 + 2 * L


def increments(below, here, above, west, east, bg):
    wx, wy, va = bg
    dx = [above[i] - below[i] for i in range(V)]
    dy = [east[i] - west[i] for i in range(V)]
    half = 0.5 * STEP
    hx, hy, sv = half * wx, half * wy, STEP * va
    inc_e = sv * here[1] - (hx * dx[0] + hy * dy[0]) - half * dx[2]
    inc_n = -(sv * here[0]) - (hx * dx[1] + hy * dy[1]) - half * dy[2]
    inc_h = -(hx * dx[2] + hy * dy[2]) - half * (dx[0] + dy[1])
    return inc_e, inc_n, inc_h


def advance(stage, start, here, inc):
    if stage == 0:
        return here + inc
    if stage == 1:
        return 0.75 * start + 0.25 * (here + inc)
    return (1.0 / 3.0) * start + (2.0 / 3.0) * (here + inc)


def lane_gather(tile, index):
    return jnp.take_along_axis(tile, index, axis=1, mode="promise_in_bounds")


def kernel(
    n_gx, n_gy, cells_all, obs_all,
    vec_ref, bg_ref, site_ref, off_ref, err_ref,
    out_ref, obs_ref,
    state, one, two, bred, bgrows, strips, edges, proj, gacc, sum_y, sum_x, part,
    send_sem, recv_sem, ysend, yrecv, xsend, xrecv,
):
    groups = site_ref.shape[0]
    gx = lax.axis_index("gx")
    gy = lax.axis_index("gy")
    up, dn = lax.rem(gx + n_gx - 1, n_gx), lax.rem(gx + 1, n_gx)
    lf, rt = lax.rem(gy + n_gy - 1, n_gy), lax.rem(gy + 1, n_gy)
    x_peers = [lax.rem(gx + d, n_gx) for d in range(1, n_gx)]
    y_peers = [lax.rem(gy + d, n_gy) for d in range(1, n_gy)]
    lane = lax.broadcasted_iota(jnp.int32, (K, COLS), 1)
    sub = lax.broadcasted_iota(jnp.int32, (K, COLS), 0)
    lane8 = lane & 7

    barrier = pltpu.get_barrier_semaphore()
    greeted = [(a, b) for a in (up, dn) for b in (lf, rt)]
    greeted += [(a, gy) for a in x_peers] + [(gx, b) for b in y_peers]
    for peer in greeted:
        pl.semaphore_signal(barrier, inc=1, device_id=peer, device_id_type=MESH)

    packed = [[jnp.zeros((K, COLS), jnp.float32) for _ in range(V + 1)] for _ in range(2)]
    for l in range(L):
        for r in range(ROWS):
            h, base = r // 4, l * 32 + (r % 4) * 8
            put = (lane >> 3) == base // 8
            for v in range(V):
                tile = vec_ref[pl.ds((v * L + l) * ROWS + r, K, stride=STRIDE), :]
                state[l, v, 4 + r] = tile
                packed[h][v] = jnp.where(put, pltpu.roll(tile, (base + 4) % COLS, 1), packed[h][v])
            rows = [
                jnp.broadcast_to(bg_ref[pl.ds((v * L + l) * ROWS + r, 1), :], (K, COLS))
                for v in range(V)
            ]
            tile = jnp.where(sub == 0, rows[0], jnp.where(sub == 1, rows[1], rows[2]))
            packed[h][V] = jnp.where(put, pltpu.roll(tile, (base + 4) % COLS, 1), packed[h][V])
        for h in range(2):
            for v in range(V):
                bgrows[1 + h, l, pl.ds(v * 4, 4), :] = bg_ref[pl.ds((v * L + l) * ROWS + h * 4, 4), :]
            bgrows[1 + h, l, pl.ds(12, 4), :] = jnp.zeros((4, COLS), jnp.float32)
    for h in range(2):
        for v in range(V + 1):
            strips[1, 1 + h, v] = packed[h][v]

    pl.semaphore_wait(barrier, len(greeted))

    def remote(src, dst, index, peer):
        return pltpu.make_async_remote_copy(
            src_ref=src, dst_ref=dst, send_sem=send_sem.at[index], recv_sem=recv_sem.at[index],
            device_id=peer, device_id_type=MESH,
        )

    both = pl.ds(1, 2)
    near = [
        remote(strips.at[1, 1], strips.at[1, 3], 0, (up, gy)),
        remote(strips.at[1, 2], strips.at[1, 0], 1, (dn, gy)),
        remote(strips.at[1, 1], strips.at[2, 3], 2, (up, lf)),
        remote(strips.at[1, 1], strips.at[0, 3], 3, (up, rt)),
        remote(strips.at[1, 2], strips.at[2, 0], 4, (dn, lf)),
        remote(strips.at[1, 2], strips.at[0, 0], 5, (dn, rt)),
        remote(strips.at[1, both], strips.at[2, both], 6, (gx, lf)),
        remote(strips.at[1, both], strips.at[0, both], 7, (gx, rt)),
        remote(bgrows.at[1], bgrows.at[3], 8, (up, gy)),
        remote(bgrows.at[2], bgrows.at[0], 9, (dn, gy)),
    ]

    def level_copies(l):
        return (
            remote(state.at[l, :, pl.ds(4, 4)], state.at[l, :, pl.ds(12, 4)], 10 + 2 * l, (up, gy)),
            remote(state.at[l, :, pl.ds(8, 4)], state.at[l, :, pl.ds(0, 4)], 11 + 2 * l, (dn, gy)),
        )

    for copy in near:
        copy.start()
    for l in range(L):
        for copy in level_copies(l):
            copy.start()

    gacc[...] = jnp.zeros_like(gacc)
    proj[...] = jnp.zeros_like(proj)
    for copy in near:
        copy.wait_recv()

    def level(l, carry):
        whole = []
        for side in range(3):
            fields = []
            for v in range(V + 1):
                tile = jnp.zeros((K, COLS), jnp.float32)
                for seg in range(4):
                    moved = pltpu.roll(strips[side, seg, v], lax.rem((seg + 4 - l) * 32, COLS), 1)
                    tile = jnp.where((lane >> 5) == seg, moved, tile)
                fields.append(tile)
            whole.append(fields)
        inner = lane8 < 4
        sides = []
        for a, b in ((0, 1), (1, 2)):
            fields = [jnp.where(inner, whole[a][v], whole[b][v]) for v in range(V + 1)]
            bg = [jnp.broadcast_to(fields[V][i : i + 1, :], (K, COLS)) for i in range(3)]
            start = fields[:V]
            here = start
            history = [start]
            for stage in range(3):
                inc = increments(
                    [pltpu.roll(f, 8, 1) for f in here], here,
                    [pltpu.roll(f, COLS - 8, 1) for f in here],
                    [pltpu.roll(f, 1, 1) for f in here],
                    [pltpu.roll(f, COLS - 1, 1) for f in here], bg,
                )
                here = [advance(stage, start[v], here[v], inc[v]) for v in range(V)]
                history.append(here)
            sides.append(history)
        for stage in range(4):
            for v in range(V):
                left, right = sides[0][stage][v], sides[1][stage][v]
                edges[stage, v] = jnp.where(
                    lane8 == 4, pltpu.roll(left, 1, 1), pltpu.roll(right, COLS - 1, 1)
                )

        for copy in level_copies(l):
            copy.wait_recv()

        def read(stage, v, q):
            if stage == 0:
                return state[l, v, q]
            return (one, two)[stage - 1][v, q]

        for stage in range(3):
            edge = [edges[stage, v] for v in range(V)]
            for q in range(1 + stage, 15 - stage):
                bg = [
                    jnp.broadcast_to(bgrows[q // 4, l, pl.ds(v * 4 + q % 4, 1), :], (K, COLS))
                    for v in range(V)
                ]
                here = [read(stage, v, q) for v in range(V)]
                rim = [pltpu.roll(edge[v], (124 - 8 * q) % COLS, 1) for v in range(V)]
                west = [jnp.where(lane == 0, rim[v], pltpu.roll(here[v], 1, 1)) for v in range(V)]
                east = [
                    jnp.where(lane == COLS - 1, rim[v], pltpu.roll(here[v], COLS - 1, 1))
                    for v in range(V)
                ]
                inc = increments(
                    [read(stage, v, q - 1) for v in range(V)], here,
                    [read(stage, v, q + 1) for v in range(V)], west, east, bg,
                )
                for v in range(V):
                    value = advance(stage, state[l, v, q], here[v], inc[v])
                    if stage == 0:
                        one[v, q] = value
                    elif stage == 1:
                        two[v, q] = value
                    else:
                        bred[l, v, q - 3] = value

        sums = [gacc[s] for s in range(SHIFTS)]
        for v in range(V):
            for rr in range(1, 9):
                tile = bred[l, v, rr]
                for s in range(SHIFTS):
                    other = tile if s == 0 else pltpu.roll(tile, K - s, 0)
                    sums[s] = sums[s] + tile * other
        for s in range(SHIFTS):
            gacc[s] = sums[s]

        def group(g, carry):
            columns = pl.ds(pl.multiple_of(g * COLS, COLS), COLS)
            site = jnp.broadcast_to(site_ref[pl.ds(g, 1), :], (K, COLS))
            a = jnp.broadcast_to(off_ref[0:1, columns], (K, COLS))
            b = jnp.broadcast_to(off_ref[1:2, columns], (K, COLS))
            plane, row, col = site >> 10, (site >> 7) & 7, site & 127
            abs_a, abs_b = jnp.abs(a), jnp.abs(b)
            row0 = jnp.where(a < 0.0, row - 1, row)
            col0 = jnp.where(b < 0.0, col - 1, col)
            wr0 = jnp.where(a < 0.0, abs_a, 1.0 - abs_a)
            wr1 = jnp.where(a < 0.0, 1.0 - abs_a, abs_a)
            wc0 = jnp.where(b < 0.0, abs_b, 1.0 - abs_b)
            wc1 = jnp.where(b < 0.0, 1.0 - abs_b, abs_b)
            past_left, past_right = col0 < 0, col0 >= COLS - 1
            w_edge = jnp.where(past_left, wc0, jnp.where(past_right, wc1, 0.0))
            wc0 = jnp.where(past_left, 0.0, wc0)
            wc1 = jnp.where(past_right, 0.0, wc1)
            at0, at1 = col0 & (COLS - 1), (col0 + 1) & (COLS - 1)
            at_edge = (row0 + 4) * 8 + jnp.where(past_left, 4, 3)
            key = (plane - l) * 16 + row0 + 1
            zero = jnp.zeros((K, COLS), jnp.float32)
            low, high, rim = zero, zero, zero
            for v in range(V):
                before = None
                for rr in range(10):
                    tile = bred[l, v, rr]
                    value = wc0 * lane_gather(tile, at0) + wc1 * lane_gather(tile, at1)
                    if before is not None:
                        high = jnp.where(before, value, high)
                    if rr < 9:
                        before = key == v * 64 + rr
                        low = jnp.where(before, value, low)
                edge = edges[3, v]
                value = wr0 * lane_gather(edge, at_edge) + wr1 * lane_gather(edge, at_edge + 8)
                rim = jnp.where(plane - l == v * 4, w_edge * value, rim)
            proj[g] += wr0 * low + wr1 * high + rim
            return carry

        lax.fori_loop(0, groups, group, 0)
        return carry

    lax.fori_loop(0, L, level, 0)

    def weigh(g, sums):
        columns = pl.ds(pl.multiple_of(g * COLS, COLS), COLS)
        tile = proj[g]
        scaled = tile / err_ref[0:1, columns]
        return tuple(
            sums[s] + scaled * (tile if s == 0 else pltpu.roll(tile, K - s, 0))
            for s in range(SHIFTS)
        )

    zero = jnp.zeros((K, COLS), jnp.float32)
    normal = lax.fori_loop(0, groups, weigh, (zero,) * SHIFTS)
    mine = zero
    for s in range(SHIFTS):
        total = gacc[s] * (1.0 / cells_all) + normal[s] * (1.0 / obs_all)
        mine = jnp.where(lane == s, jnp.sum(total, axis=1, keepdims=True), mine)

    def all_sum(value, slots, me, peers, device, sends, recvs):
        part[...] = value
        slots[me] = value
        copies = [
            pltpu.make_async_remote_copy(
                src_ref=part, dst_ref=slots.at[me], send_sem=sends.at[d], recv_sem=recvs.at[d],
                device_id=device(peer), device_id_type=MESH,
            )
            for d, peer in enumerate(peers)
        ]
        for copy in copies:
            copy.start()
        for copy in copies:
            copy.wait()
        total = slots[0]
        for i in range(1, len(peers) + 1):
            total = total + slots[i]
        return total

    mine = all_sum(mine, sum_y, gy, y_peers, lambda p: (gx, p), ysend, yrecv)
    mine = all_sum(mine, sum_x, gx, x_peers, lambda p: (p, gy), xsend, xrecv)

    matrix = jnp.where(lane == sub + K, 1.0, 0.0)
    for s in range(K):
        if s < SHIFTS:
            diagonal = mine[:, s : s + 1]
        else:
            diagonal = pltpu.roll(mine, K - s, 0)[:, K - s : K - s + 1]
        matrix = jnp.where((lane < K) & (((lane - sub) & 7) == s), diagonal, matrix)
    scale = jnp.ones((K, COLS), jnp.float32)
    for j in range(K):
        pivot_row = jnp.broadcast_to(matrix[j : j + 1, :], (K, COLS))
        pivot = jnp.broadcast_to(pivot_row[:, j : j + 1], (K, COLS))
        column = jnp.broadcast_to(matrix[:, j : j + 1], (K, COLS))
        scale = jnp.where(sub == j, pivot, scale)
        matrix = jnp.where(sub > j, matrix - (column / pivot) * pivot_row, matrix)
    matrix = matrix / jnp.sqrt(scale)
    combo = [jnp.broadcast_to(matrix[:, K + j : K + j + 1], (K, COLS)) for j in range(K)]

    def mix(tile):
        terms = [combo[j] * jnp.broadcast_to(tile[j : j + 1, :], (K, COLS)) for j in range(K)]
        while len(terms) > 1:
            terms = [terms[i] + terms[i + 1] for i in range(0, len(terms), 2)]
        return terms[0]

    def write(l, carry):
        for v in range(V):
            for r in range(ROWS):
                out_ref[pl.ds(v * L * ROWS + l * ROWS + r, K, stride=STRIDE), :] = mix(bred[l, v, r + 1])
        return carry

    lax.fori_loop(0, L, write, 0)

    def write_obs(g, carry):
        columns = pl.ds(pl.multiple_of(g * COLS, COLS), COLS)
        obs_ref[:, columns] = mix(proj[g]) / jnp.sqrt(err_ref[0:1, columns])
        return carry

    lax.fori_loop(0, groups, write_obs, 0)
    for copy in near:
        copy.wait_send()
    for l in range(L):
        for copy in level_copies(l):
            copy.wait_send()


def local(n_gx, n_gy, vectors, background, obs_site, obs_offset, obs_error):
    obs_dev = obs_site.shape[0]
    groups = obs_dev // COLS
    devices = n_gx * n_gy
    body = functools.partial(
        kernel, n_gx, n_gy, float(PLANES * ROWS * COLS * devices), float(obs_dev * devices)
    )
    f32 = jnp.float32
    vmem = pl.BlockSpec(memory_space=pltpu.VMEM)
    analysis, obs = pl.pallas_call(
        body,
        out_shape=(
            jax.ShapeDtypeStruct((K * STRIDE, COLS), f32),
            jax.ShapeDtypeStruct((K, obs_dev), f32),
        ),
        in_specs=[vmem] * 5,
        out_specs=(vmem, vmem),
        scratch_shapes=[
            pltpu.VMEM((L, V, 16, K, COLS), f32),
            pltpu.VMEM((V, 16, K, COLS), f32),
            pltpu.VMEM((V, 16, K, COLS), f32),
            pltpu.VMEM((L, V, 10, K, COLS), f32),
            pltpu.VMEM((4, L, 16, COLS), f32),
            pltpu.VMEM((3, 4, V + 1, K, COLS), f32),
            pltpu.VMEM((4, V, K, COLS), f32),
            pltpu.VMEM((groups, K, COLS), f32),
            pltpu.VMEM((SHIFTS, K, COLS), f32),
            pltpu.VMEM((n_gy, K, COLS), f32),
            pltpu.VMEM((n_gx, K, COLS), f32),
            pltpu.VMEM((K, COLS), f32),
            pltpu.SemaphoreType.DMA((N_COPIES,)),
            pltpu.SemaphoreType.DMA((N_COPIES,)),
            pltpu.SemaphoreType.DMA((n_gy - 1,)),
            pltpu.SemaphoreType.DMA((n_gy - 1,)),
            pltpu.SemaphoreType.DMA((n_gx - 1,)),
            pltpu.SemaphoreType.DMA((n_gx - 1,)),
        ],
        compiler_params=pltpu.CompilerParams(
            collective_id=0, has_side_effects=True, vmem_limit_bytes=24 * 1024 * 1024
        ),
    )(
        vectors.reshape(K * STRIDE, COLS),
        background.reshape(V * L * ROWS, COLS),
        obs_site.reshape(groups, COLS),
        obs_offset,
        obs_error.reshape(1, obs_dev),
    )
    return analysis.reshape(vectors.shape), obs


def solution(mesh):
    placed = (
        P(None, None, None, "gx", "gy"),
        P(None, None, "gx", "gy"),
        P(("gx", "gy")),
        P(None, ("gx", "gy")),
        P(("gx", "gy")),
    )
    return jax.shard_map(
        functools.partial(local, mesh.shape["gx"], mesh.shape["gy"]),
        mesh=mesh,
        in_specs=placed,
        out_specs=(P(None, None, None, "gx", "gy"), P(None, ("gx", "gy"))),
        check_vma=False,
    )
```

```python
import functools

import jax
import jax.numpy as jnp
from jax import lax
from jax.experimental import pallas as pl
from jax.experimental.pallas import tpu as pltpu
from jax.sharding import PartitionSpec as P

K = 8
V = 3
L = 4
ROWS = 8
COLS = 128
PLANES = V * L
STRIDE = PLANES * ROWS
STEP = 0.35
MESH = pl.DeviceIdType.MESH
SHIFTS = 5
N_EDGE = 8
M_ROWS = V * 10 * K
WIDE = 512
N_COPIES = N_EDGE + 2 + 2 * L


def increments(below, here, above, west, east, bg):
    wx, wy, va = bg
    dx = [above[i] - below[i] for i in range(V)]
    dy = [east[i] - west[i] for i in range(V)]
    half = 0.5 * STEP
    hx, hy, sv = half * wx, half * wy, STEP * va
    inc_e = sv * here[1] - (hx * dx[0] + hy * dy[0]) - half * dx[2]
    inc_n = -(sv * here[0]) - (hx * dx[1] + hy * dy[1]) - half * dy[2]
    inc_h = -(hx * dx[2] + hy * dy[2]) - half * (dx[0] + dy[1])
    return inc_e, inc_n, inc_h


def advance(stage, start, here, inc):
    if stage == 0:
        return here + inc
    if stage == 1:
        return 0.75 * start + 0.25 * (here + inc)
    return (1.0 / 3.0) * start + (2.0 / 3.0) * (here + inc)


def split(value):
    high = value.astype(jnp.bfloat16).astype(jnp.float32)
    return high, value - high


def kernel(
    n_gx, n_gy, cells_all, obs_all,
    vec_hbm, bg_hbm, site_hbm, off_hbm, err_hbm,
    out_hbm, obs_hbm,
    out_ref, obs_ref, store_sem,
    vec_ref, bg_ref, site_ref, off_ref, err_ref, load_sem,
    weights, lhs, seams, keys, row_w,
    state, one, two, bred, bgrows, strips, edges, proj, gacc, sum_y, sum_x, part,
    send_sem, recv_sem, ysend, yrecv, xsend, xrecv,
):
    groups = proj.shape[0]
    gx = lax.axis_index("gx")
    gy = lax.axis_index("gy")
    up, dn = lax.rem(gx + n_gx - 1, n_gx), lax.rem(gx + 1, n_gx)
    lf, rt = lax.rem(gy + n_gy - 1, n_gy), lax.rem(gy + 1, n_gy)
    x_peers = [lax.rem(gx + d, n_gx) for d in range(1, n_gx)]
    y_peers = [lax.rem(gy + d, n_gy) for d in range(1, n_gy)]
    lane = lax.broadcasted_iota(jnp.int32, (K, COLS), 1)
    sub = lax.broadcasted_iota(jnp.int32, (K, COLS), 0)
    lane8 = lane & 7

    loads = [
        pltpu.make_async_copy(src, dst, load_sem.at[i])
        for i, (src, dst) in enumerate(
            [(bg_hbm, bg_ref), (vec_hbm, vec_ref), (site_hbm, site_ref),
             (off_hbm, off_ref), (err_hbm, err_ref)]
        )
    ]
    for copy in loads:
        copy.start()

    barrier = pltpu.get_barrier_semaphore()
    greeted = [(a, b) for a in (up, dn) for b in (lf, rt)]
    greeted += [(a, gy) for a in x_peers] + [(gx, b) for b in y_peers]
    for peer in greeted:
        pl.semaphore_signal(barrier, inc=1, device_id=peer, device_id_type=MESH)

    loads[0].wait()
    loads[1].wait()
    packed = [[jnp.zeros((K, COLS), jnp.float32) for _ in range(V + 1)] for _ in range(2)]
    for l in range(L):
        for r in range(ROWS):
            h, base = r // 4, l * 32 + (r % 4) * 8
            put = (lane >> 3) == base // 8
            for v in range(V):
                tile = vec_ref[pl.ds((v * L + l) * ROWS + r, K, stride=STRIDE), :]
                state[l, v, 4 + r] = tile
                packed[h][v] = jnp.where(put, pltpu.roll(tile, (base + 4) % COLS, 1), packed[h][v])
            rows = [
                jnp.broadcast_to(bg_ref[pl.ds((v * L + l) * ROWS + r, 1), :], (K, COLS))
                for v in range(V)
            ]
            tile = jnp.where(sub == 0, rows[0], jnp.where(sub == 1, rows[1], rows[2]))
            packed[h][V] = jnp.where(put, pltpu.roll(tile, (base + 4) % COLS, 1), packed[h][V])
        for h in range(2):
            for v in range(V):
                bgrows[1 + h, l, pl.ds(v * 4, 4), :] = bg_ref[pl.ds((v * L + l) * ROWS + h * 4, 4), :]
            bgrows[1 + h, l, pl.ds(12, 4), :] = jnp.zeros((4, COLS), jnp.float32)
    for h in range(2):
        for v in range(V + 1):
            strips[1, 1 + h, v] = packed[h][v]

    pl.semaphore_wait(barrier, len(greeted))

    def remote(src, dst, index, peer):
        return pltpu.make_async_remote_copy(
            src_ref=src, dst_ref=dst, send_sem=send_sem.at[index], recv_sem=recv_sem.at[index],
            device_id=peer, device_id_type=MESH,
        )

    both = pl.ds(1, 2)
    near = [
        remote(strips.at[1, 1], strips.at[1, 3], 0, (up, gy)),
        remote(strips.at[1, 2], strips.at[1, 0], 1, (dn, gy)),
        remote(strips.at[1, 1], strips.at[2, 3], 2, (up, lf)),
        remote(strips.at[1, 1], strips.at[0, 3], 3, (up, rt)),
        remote(strips.at[1, 2], strips.at[2, 0], 4, (dn, lf)),
        remote(strips.at[1, 2], strips.at[0, 0], 5, (dn, rt)),
        remote(strips.at[1, both], strips.at[2, both], 6, (gx, lf)),
        remote(strips.at[1, both], strips.at[0, both], 7, (gx, rt)),
        remote(bgrows.at[1], bgrows.at[3], 8, (up, gy)),
        remote(bgrows.at[2], bgrows.at[0], 9, (dn, gy)),
    ]

    def level_copies(l):
        return (
            remote(state.at[l, :, pl.ds(4, 4)], state.at[l, :, pl.ds(12, 4)], 10 + 2 * l, (up, gy)),
            remote(state.at[l, :, pl.ds(8, 4)], state.at[l, :, pl.ds(0, 4)], 11 + 2 * l, (dn, gy)),
        )

    for copy in near:
        copy.start()
    for l in range(L):
        for copy in level_copies(l):
            copy.start()

    gacc[...] = jnp.zeros_like(gacc)
    proj[...] = jnp.zeros_like(proj)
    for copy in loads[2:]:
        copy.wait()

    cell = lax.broadcasted_iota(jnp.int32, (COLS, COLS), 0)
    slot = lax.broadcasted_iota(jnp.int32, (16, COLS), 0)
    weights[pl.ds(3 * COLS, COLS), :] = jnp.zeros((COLS, groups * COLS), jnp.bfloat16)

    def weigh_columns(g, carry):
        columns = pl.ds(pl.multiple_of(g * COLS, COLS), COLS)
        site = site_ref[pl.ds(g, 1), :]
        a, b = off_ref[0:1, columns], off_ref[1:2, columns]
        row, col = (site >> 7) & 7, site & 127
        abs_a, abs_b = jnp.abs(a), jnp.abs(b)
        row0 = jnp.where(a < 0.0, row - 1, row)
        col0 = jnp.where(b < 0.0, col - 1, col)
        keys[g] = jnp.broadcast_to((site >> 10) * 16 + row0 + 1, (K, COLS))
        row_w[g, 0] = jnp.broadcast_to(jnp.where(a < 0.0, abs_a, 1.0 - abs_a), (K, COLS))
        row_w[g, 1] = jnp.broadcast_to(jnp.where(a < 0.0, 1.0 - abs_a, abs_a), (K, COLS))
        w0 = jnp.where(b < 0.0, abs_b, 1.0 - abs_b)
        w1 = jnp.where(b < 0.0, 1.0 - abs_b, abs_b)
        high, low = split(
            jnp.where(cell == col0, w0, 0.0) + jnp.where(cell == col0 + 1, w1, 0.0)
        )
        weights[pl.ds(0, COLS), columns] = high.astype(jnp.bfloat16)
        weights[pl.ds(COLS, COLS), columns] = high.astype(jnp.bfloat16)
        weights[pl.ds(2 * COLS, COLS), columns] = low.astype(jnp.bfloat16)
        at_left = jnp.where(col0 < 0, w0, 0.0)
        at_right = jnp.where(col0 >= COLS - 1, w1, 0.0)
        high, low = split(jnp.where((slot & 1) == 0, at_right, at_left))
        seam = jnp.where(slot < 4, high, jnp.where(slot < 6, low, 0.0))
        weights[pl.ds(3 * COLS, 16), columns] = seam.astype(jnp.bfloat16)
        return carry

    lax.fori_loop(0, groups, weigh_columns, 0)
    for copy in near:
        copy.wait_recv()

    def level(l, carry):
        whole = []
        for side in range(3):
            fields = []
            for v in range(V + 1):
                tile = jnp.zeros((K, COLS), jnp.float32)
                for seg in range(4):
                    moved = pltpu.roll(strips[side, seg, v], lax.rem((seg + 4 - l) * 32, COLS), 1)
                    tile = jnp.where((lane >> 5) == seg, moved, tile)
                fields.append(tile)
            whole.append(fields)
        inner = lane8 < 4
        sides = []
        for a, b in ((0, 1), (1, 2)):
            fields = [jnp.where(inner, whole[a][v], whole[b][v]) for v in range(V + 1)]
            bg = [jnp.broadcast_to(fields[V][i : i + 1, :], (K, COLS)) for i in range(3)]
            start = fields[:V]
            here = start
            history = [start]
            for stage in range(3):
                inc = increments(
                    [pltpu.roll(f, 8, 1) for f in here], here,
                    [pltpu.roll(f, COLS - 8, 1) for f in here],
                    [pltpu.roll(f, 1, 1) for f in here],
                    [pltpu.roll(f, COLS - 1, 1) for f in here], bg,
                )
                here = [advance(stage, start[v], here[v], inc[v]) for v in range(V)]
                history.append(here)
            sides.append(history)
        for stage in range(4):
            for v in range(V):
                left, right = sides[0][stage][v], sides[1][stage][v]
                edges[stage, v] = jnp.where(
                    lane8 == 4, pltpu.roll(left, 1, 1), pltpu.roll(right, COLS - 1, 1)
                )

        for copy in level_copies(l):
            copy.wait_recv()

        def read(stage, v, q):
            if stage == 0:
                return state[l, v, q]
            return (one, two)[stage - 1][v, q]

        for stage in range(3):
            edge = [edges[stage, v] for v in range(V)]
            for q in range(1 + stage, 15 - stage):
                bg = [
                    jnp.broadcast_to(bgrows[q // 4, l, pl.ds(v * 4 + q % 4, 1), :], (K, COLS))
                    for v in range(V)
                ]
                here = [read(stage, v, q) for v in range(V)]
                rim = [pltpu.roll(edge[v], (124 - 8 * q) % COLS, 1) for v in range(V)]
                west = [jnp.where(lane == 0, rim[v], pltpu.roll(here[v], 1, 1)) for v in range(V)]
                east = [
                    jnp.where(lane == COLS - 1, rim[v], pltpu.roll(here[v], COLS - 1, 1))
                    for v in range(V)
                ]
                inc = increments(
                    [read(stage, v, q - 1) for v in range(V)], here,
                    [read(stage, v, q + 1) for v in range(V)], west, east, bg,
                )
                for v in range(V):
                    value = advance(stage, state[l, v, q], here[v], inc[v])
                    if stage == 0:
                        one[v, q] = value
                    elif stage == 1:
                        two[v, q] = value
                    else:
                        bred[l, v, q - 3] = value

        sums = [gacc[s] for s in range(SHIFTS)]
        for v in range(V):
            for rr in range(1, 9):
                tile = bred[l, v, rr]
                for s in range(SHIFTS):
                    other = tile if s == 0 else pltpu.roll(tile, K - s, 0)
                    sums[s] = sums[s] + tile * other
        for s in range(SHIFTS):
            gacc[s] = sums[s]

        for v in range(V):
            high, low = split(edges[3, v])
            slots = jnp.where(
                (lane8 == 3) | (lane8 == 4), high,
                jnp.where((lane8 == 5) | (lane8 == 6), pltpu.roll(low, 2, 1), pltpu.roll(high, 4, 1)),
            )
            for rr in range(10):
                moved = pltpu.roll(slots, COLS - 8 * (rr + 3) - 3, 1)
                seams[v, rr] = jnp.where(lane < 6, moved, 0.0)
        high, low = split(bred[l].reshape(M_ROWS, COLS))
        lhs[:, 0:COLS] = high.astype(jnp.bfloat16)
        lhs[:, COLS : 2 * COLS] = low.astype(jnp.bfloat16)
        lhs[:, 2 * COLS : 3 * COLS] = high.astype(jnp.bfloat16)
        lhs[:, 3 * COLS :] = seams[...].reshape(M_ROWS, COLS).astype(jnp.bfloat16)

        def block(n, carry):
            columns = pl.ds(pl.multiple_of(n * WIDE, WIDE), WIDE)
            mixed = jnp.dot(lhs[...], weights[:, columns], preferred_element_type=jnp.float32)
            for i in range(WIDE // COLS):
                g = n * (WIDE // COLS) + i
                key = keys[g] - l * 16
                low = jnp.zeros((K, COLS), jnp.float32)
                high = low
                for v in range(V):
                    before = None
                    for rr in range(10):
                        at = (v * 10 + rr) * K
                        value = mixed[at : at + K, i * COLS : (i + 1) * COLS]
                        if before is not None:
                            high = jnp.where(before, value, high)
                        if rr < 9:
                            before = key == v * 64 + rr
                            low = jnp.where(before, value, low)
                proj[g] += row_w[g, 0] * low + row_w[g, 1] * high
            return carry

        lax.fori_loop(0, groups * COLS // WIDE, block, 0)
        return carry

    lax.fori_loop(0, L, level, 0)

    def weigh(g, sums):
        columns = pl.ds(pl.multiple_of(g * COLS, COLS), COLS)
        tile = proj[g]
        scaled = tile / err_ref[0:1, columns]
        return tuple(
            sums[s] + scaled * (tile if s == 0 else pltpu.roll(tile, K - s, 0))
            for s in range(SHIFTS)
        )

    zero = jnp.zeros((K, COLS), jnp.float32)
    normal = lax.fori_loop(0, groups, weigh, (zero,) * SHIFTS)
    mine = zero
    for s in range(SHIFTS):
        total = gacc[s] * (1.0 / cells_all) + normal[s] * (1.0 / obs_all)
        mine = jnp.where(lane == s, jnp.sum(total, axis=1, keepdims=True), mine)

    def all_sum(value, slots, me, peers, device, sends, recvs):
        part[...] = value
        slots[me] = value
        copies = [
            pltpu.make_async_remote_copy(
                src_ref=part, dst_ref=slots.at[me], send_sem=sends.at[d], recv_sem=recvs.at[d],
                device_id=device(peer), device_id_type=MESH,
            )
            for d, peer in enumerate(peers)
        ]
        for copy in copies:
            copy.start()
        for copy in copies:
            copy.wait()
        total = slots[0]
        for i in range(1, len(peers) + 1):
            total = total + slots[i]
        return total

    mine = all_sum(mine, sum_y, gy, y_peers, lambda p: (gx, p), ysend, yrecv)
    mine = all_sum(mine, sum_x, gx, x_peers, lambda p: (p, gy), xsend, xrecv)

    matrix = jnp.where(lane == sub + K, 1.0, 0.0)
    for s in range(K):
        if s < SHIFTS:
            diagonal = mine[:, s : s + 1]
        else:
            diagonal = pltpu.roll(mine, K - s, 0)[:, K - s : K - s + 1]
        matrix = jnp.where((lane < K) & (((lane - sub) & 7) == s), diagonal, matrix)
    scale = jnp.ones((K, COLS), jnp.float32)
    for j in range(K):
        pivot_row = jnp.broadcast_to(matrix[j : j + 1, :], (K, COLS))
        pivot = jnp.broadcast_to(pivot_row[:, j : j + 1], (K, COLS))
        column = jnp.broadcast_to(matrix[:, j : j + 1], (K, COLS))
        scale = jnp.where(sub == j, pivot, scale)
        matrix = jnp.where(sub > j, matrix - (column / pivot) * pivot_row, matrix)
    matrix = matrix / jnp.sqrt(scale)
    combo = [jnp.broadcast_to(matrix[:, K + j : K + j + 1], (K, COLS)) for j in range(K)]

    def mix(tile):
        terms = [combo[j] * jnp.broadcast_to(tile[j : j + 1, :], (K, COLS)) for j in range(K)]
        while len(terms) > 1:
            terms = [terms[i] + terms[i + 1] for i in range(0, len(terms), 2)]
        return terms[0]

    def write_obs(g, carry):
        columns = pl.ds(pl.multiple_of(g * COLS, COLS), COLS)
        obs_ref[:, columns] = mix(proj[g]) / jnp.sqrt(err_ref[0:1, columns])
        return carry

    lax.fori_loop(0, groups, write_obs, 0)
    obs_out = pltpu.make_async_copy(obs_ref, obs_hbm, store_sem.at[0])
    obs_out.start()

    def write(l, carry):
        for v in range(V):
            for r in range(ROWS):
                out_ref[pl.ds(v * L * ROWS + l * ROWS + r, K, stride=STRIDE), :] = mix(bred[l, v, r + 1])
        return carry

    lax.fori_loop(0, L, write, 0)

    out = pltpu.make_async_copy(out_ref, out_hbm, store_sem.at[1])
    out.start()
    for copy in near:
        copy.wait_send()
    for l in range(L):
        for copy in level_copies(l):
            copy.wait_send()
    obs_out.wait()
    out.wait()


def local(n_gx, n_gy, vectors, background, obs_site, obs_offset, obs_error):
    obs_dev = obs_site.shape[0]
    groups = obs_dev // COLS
    devices = n_gx * n_gy
    body = functools.partial(
        kernel, n_gx, n_gy, float(PLANES * ROWS * COLS * devices), float(obs_dev * devices)
    )
    f32 = jnp.float32
    hbm = pl.BlockSpec(memory_space=pltpu.HBM)
    analysis, obs = pl.pallas_call(
        body,
        out_shape=(
            jax.ShapeDtypeStruct((K * STRIDE, COLS), f32),
            jax.ShapeDtypeStruct((K, obs_dev), f32),
        ),
        in_specs=[hbm] * 5,
        out_specs=(hbm, hbm),
        scratch_shapes=[
            pltpu.VMEM((K * STRIDE, COLS), f32),
            pltpu.VMEM((K, obs_dev), f32),
            pltpu.SemaphoreType.DMA((2,)),
            pltpu.VMEM((K * STRIDE, COLS), f32),
            pltpu.VMEM((V * L * ROWS, COLS), f32),
            pltpu.VMEM((groups, COLS), jnp.int32),
            pltpu.VMEM((2, obs_dev), f32),
            pltpu.VMEM((1, obs_dev), f32),
            pltpu.SemaphoreType.DMA((5,)),
            pltpu.VMEM((4 * COLS, obs_dev), jnp.bfloat16),
            pltpu.VMEM((M_ROWS, 4 * COLS), jnp.bfloat16),
            pltpu.VMEM((V, 10, K, COLS), f32),
            pltpu.VMEM((groups, K, COLS), jnp.int32),
            pltpu.VMEM((groups, 2, K, COLS), f32),
            pltpu.VMEM((L, V, 16, K, COLS), f32),
            pltpu.VMEM((V, 16, K, COLS), f32),
            pltpu.VMEM((V, 16, K, COLS), f32),
            pltpu.VMEM((L, V, 10, K, COLS), f32),
            pltpu.VMEM((4, L, 16, COLS), f32),
            pltpu.VMEM((3, 4, V + 1, K, COLS), f32),
            pltpu.VMEM((4, V, K, COLS), f32),
            pltpu.VMEM((groups, K, COLS), f32),
            pltpu.VMEM((SHIFTS, K, COLS), f32),
            pltpu.VMEM((n_gy, K, COLS), f32),
            pltpu.VMEM((n_gx, K, COLS), f32),
            pltpu.VMEM((K, COLS), f32),
            pltpu.SemaphoreType.DMA((N_COPIES,)),
            pltpu.SemaphoreType.DMA((N_COPIES,)),
            pltpu.SemaphoreType.DMA((n_gy - 1,)),
            pltpu.SemaphoreType.DMA((n_gy - 1,)),
            pltpu.SemaphoreType.DMA((n_gx - 1,)),
            pltpu.SemaphoreType.DMA((n_gx - 1,)),
        ],
        compiler_params=pltpu.CompilerParams(
            collective_id=0, has_side_effects=True, vmem_limit_bytes=63 * 1024 * 1024
        ),
    )(
        vectors.reshape(K * STRIDE, COLS),
        background.reshape(V * L * ROWS, COLS),
        obs_site.reshape(groups, COLS),
        obs_offset,
        obs_error.reshape(1, obs_dev),
    )
    return analysis.reshape(vectors.shape), obs


def solution(mesh):
    placed = (
        P(None, None, None, "gx", "gy"),
        P(None, None, "gx", "gy"),
        P(("gx", "gy")),
        P(None, ("gx", "gy")),
        P(("gx", "gy")),
    )
    return jax.shard_map(
        functools.partial(local, mesh.shape["gx"], mesh.shape["gy"]),
        mesh=mesh,
        in_specs=placed,
        out_specs=(P(None, None, None, "gx", "gy"), P(None, ("gx", "gy"))),
        check_vma=False,
    )
```

```python
import functools

import jax
import jax.numpy as jnp
from jax import lax
from jax.experimental import pallas as pl
from jax.experimental.pallas import tpu as pltpu
from jax.sharding import PartitionSpec as P

K = 8
V = 3
L = 4
ROWS = 8
COLS = 128
PLANES = V * L
STRIDE = PLANES * ROWS
STEP = 0.35
MESH = pl.DeviceIdType.MESH
SHIFTS = 5
N_EDGE = 8
M_ROWS = V * 10 * K
WIDE = 256
N_COPIES = N_EDGE + 2 + 2 * L


def increments(below, here, above, west, east, bg):
    wx, wy, va = bg
    dx = [above[i] - below[i] for i in range(V)]
    dy = [east[i] - west[i] for i in range(V)]
    half = 0.5 * STEP
    hx, hy, sv = half * wx, half * wy, STEP * va
    inc_e = sv * here[1] - (hx * dx[0] + hy * dy[0]) - half * dx[2]
    inc_n = -(sv * here[0]) - (hx * dx[1] + hy * dy[1]) - half * dy[2]
    inc_h = -(hx * dx[2] + hy * dy[2]) - half * (dx[0] + dy[1])
    return inc_e, inc_n, inc_h


def advance(stage, start, here, inc):
    if stage == 0:
        return here + inc
    if stage == 1:
        return 0.75 * start + 0.25 * (here + inc)
    return (1.0 / 3.0) * start + (2.0 / 3.0) * (here + inc)


def split(value):
    high = value.astype(jnp.bfloat16).astype(jnp.float32)
    return high, value - high


def kernel(
    n_gx, n_gy, cells_all, obs_all,
    vec_hbm, bg_hbm, site_hbm, off_hbm, err_hbm,
    out_hbm, obs_hbm,
    out_ref, obs_ref, store_sem,
    vec_ref, bg_ref, site_ref, off_ref, err_ref, load_sem,
    weights, lhs, seams, keys, row_w,
    state, one, two, bred, bgrows, strips, edges, proj, gacc, sum_y, sum_x, part,
    send_sem, recv_sem, ysend, yrecv, xsend, xrecv,
):
    groups = proj.shape[0]
    gx = lax.axis_index("gx")
    gy = lax.axis_index("gy")
    up, dn = lax.rem(gx + n_gx - 1, n_gx), lax.rem(gx + 1, n_gx)
    lf, rt = lax.rem(gy + n_gy - 1, n_gy), lax.rem(gy + 1, n_gy)
    x_peers = [lax.rem(gx + d, n_gx) for d in range(1, n_gx)]
    y_peers = [lax.rem(gy + d, n_gy) for d in range(1, n_gy)]
    lane = lax.broadcasted_iota(jnp.int32, (K, COLS), 1)
    sub = lax.broadcasted_iota(jnp.int32, (K, COLS), 0)
    lane8 = lane & 7

    loads = [
        pltpu.make_async_copy(src, dst, load_sem.at[i])
        for i, (src, dst) in enumerate(
            [(bg_hbm, bg_ref), (vec_hbm, vec_ref), (site_hbm, site_ref),
             (off_hbm, off_ref), (err_hbm, err_ref)]
        )
    ]
    for copy in loads:
        copy.start()

    barrier = pltpu.get_barrier_semaphore()
    greeted = [(a, b) for a in (up, dn) for b in (lf, rt)]
    greeted += [(a, gy) for a in x_peers] + [(gx, b) for b in y_peers]
    for peer in greeted:
        pl.semaphore_signal(barrier, inc=1, device_id=peer, device_id_type=MESH)

    loads[0].wait()
    loads[1].wait()
    packed = [[jnp.zeros((K, COLS), jnp.float32) for _ in range(V + 1)] for _ in range(2)]
    for l in range(L):
        for r in range(ROWS):
            h, base = r // 4, l * 32 + (r % 4) * 8
            put = (lane >> 3) == base // 8
            for v in range(V):
                tile = vec_ref[pl.ds((v * L + l) * ROWS + r, K, stride=STRIDE), :]
                state[l, v, 4 + r] = tile
                packed[h][v] = jnp.where(put, pltpu.roll(tile, (base + 4) % COLS, 1), packed[h][v])
            rows = [
                jnp.broadcast_to(bg_ref[pl.ds((v * L + l) * ROWS + r, 1), :], (K, COLS))
                for v in range(V)
            ]
            tile = jnp.where(sub == 0, rows[0], jnp.where(sub == 1, rows[1], rows[2]))
            packed[h][V] = jnp.where(put, pltpu.roll(tile, (base + 4) % COLS, 1), packed[h][V])
        for h in range(2):
            for v in range(V):
                bgrows[1 + h, l, pl.ds(v * 4, 4), :] = bg_ref[pl.ds((v * L + l) * ROWS + h * 4, 4), :]
            bgrows[1 + h, l, pl.ds(12, 4), :] = jnp.zeros((4, COLS), jnp.float32)
    for h in range(2):
        for v in range(V + 1):
            strips[1, 1 + h, v] = packed[h][v]

    pl.semaphore_wait(barrier, len(greeted))

    def remote(src, dst, index, peer):
        return pltpu.make_async_remote_copy(
            src_ref=src, dst_ref=dst, send_sem=send_sem.at[index], recv_sem=recv_sem.at[index],
            device_id=peer, device_id_type=MESH,
        )

    both = pl.ds(1, 2)
    near = [
        remote(strips.at[1, 1], strips.at[1, 3], 0, (up, gy)),
        remote(strips.at[1, 2], strips.at[1, 0], 1, (dn, gy)),
        remote(strips.at[1, 1], strips.at[2, 3], 2, (up, lf)),
        remote(strips.at[1, 1], strips.at[0, 3], 3, (up, rt)),
        remote(strips.at[1, 2], strips.at[2, 0], 4, (dn, lf)),
        remote(strips.at[1, 2], strips.at[0, 0], 5, (dn, rt)),
        remote(strips.at[1, both], strips.at[2, both], 6, (gx, lf)),
        remote(strips.at[1, both], strips.at[0, both], 7, (gx, rt)),
        remote(bgrows.at[1], bgrows.at[3], 8, (up, gy)),
        remote(bgrows.at[2], bgrows.at[0], 9, (dn, gy)),
    ]

    def level_copies(l):
        return (
            remote(state.at[l, :, pl.ds(4, 4)], state.at[l, :, pl.ds(12, 4)], 10 + 2 * l, (up, gy)),
            remote(state.at[l, :, pl.ds(8, 4)], state.at[l, :, pl.ds(0, 4)], 11 + 2 * l, (dn, gy)),
        )

    for copy in near:
        copy.start()
    for l in range(L):
        for copy in level_copies(l):
            copy.start()

    gacc[...] = jnp.zeros_like(gacc)
    proj[...] = jnp.zeros_like(proj)
    for copy in loads[2:]:
        copy.wait()

    cell = lax.broadcasted_iota(jnp.int32, (COLS, COLS), 0)
    slot = lax.broadcasted_iota(jnp.int32, (16, COLS), 0)
    weights[pl.ds(3 * COLS, COLS), :] = jnp.zeros((COLS, groups * COLS), jnp.bfloat16)

    def weigh_columns(g, carry):
        columns = pl.ds(pl.multiple_of(g * COLS, COLS), COLS)
        site = site_ref[pl.ds(g, 1), :]
        a, b = off_ref[0:1, columns], off_ref[1:2, columns]
        row, col = (site >> 7) & 7, site & 127
        abs_a, abs_b = jnp.abs(a), jnp.abs(b)
        row0 = jnp.where(a < 0.0, row - 1, row)
        col0 = jnp.where(b < 0.0, col - 1, col)
        keys[g] = jnp.broadcast_to((site >> 10) * 16 + row0 + 1, (K, COLS))
        row_w[g, 0] = jnp.broadcast_to(jnp.where(a < 0.0, abs_a, 1.0 - abs_a), (K, COLS))
        row_w[g, 1] = jnp.broadcast_to(jnp.where(a < 0.0, 1.0 - abs_a, abs_a), (K, COLS))
        w0 = jnp.where(b < 0.0, abs_b, 1.0 - abs_b)
        w1 = jnp.where(b < 0.0, 1.0 - abs_b, abs_b)
        high, low = split(
            jnp.where(cell == col0, w0, 0.0) + jnp.where(cell == col0 + 1, w1, 0.0)
        )
        weights[pl.ds(0, COLS), columns] = high.astype(jnp.bfloat16)
        weights[pl.ds(COLS, COLS), columns] = high.astype(jnp.bfloat16)
        weights[pl.ds(2 * COLS, COLS), columns] = low.astype(jnp.bfloat16)
        at_left = jnp.where(col0 < 0, w0, 0.0)
        at_right = jnp.where(col0 >= COLS - 1, w1, 0.0)
        high, low = split(jnp.where((slot & 1) == 0, at_right, at_left))
        seam = jnp.where(slot < 4, high, jnp.where(slot < 6, low, 0.0))
        weights[pl.ds(3 * COLS, 16), columns] = seam.astype(jnp.bfloat16)
        return carry

    lax.fori_loop(0, groups, weigh_columns, 0)
    for copy in near:
        copy.wait_recv()

    for l in range(L):
        whole = []
        for side in range(3):
            fields = []
            for v in range(V + 1):
                tile = jnp.zeros((K, COLS), jnp.float32)
                for seg in range(4):
                    moved = pltpu.roll(strips[side, seg, v], (seg + 4 - l) * 32 % COLS, 1)
                    tile = jnp.where((lane >> 5) == seg, moved, tile)
                fields.append(tile)
            whole.append(fields)
        inner = lane8 < 4
        sides = []
        for a, b in ((0, 1), (1, 2)):
            fields = [jnp.where(inner, whole[a][v], whole[b][v]) for v in range(V + 1)]
            bg = [jnp.broadcast_to(fields[V][i : i + 1, :], (K, COLS)) for i in range(3)]
            start = fields[:V]
            here = start
            history = [start]
            for stage in range(3):
                inc = increments(
                    [pltpu.roll(f, 8, 1) for f in here], here,
                    [pltpu.roll(f, COLS - 8, 1) for f in here],
                    [pltpu.roll(f, 1, 1) for f in here],
                    [pltpu.roll(f, COLS - 1, 1) for f in here], bg,
                )
                here = [advance(stage, start[v], here[v], inc[v]) for v in range(V)]
                history.append(here)
            sides.append(history)
        for stage in range(4):
            for v in range(V):
                left, right = sides[0][stage][v], sides[1][stage][v]
                edges[l, stage, v] = jnp.where(
                    lane8 == 4, pltpu.roll(left, 1, 1), pltpu.roll(right, COLS - 1, 1)
                )

    def level(l, carry):
        for copy in level_copies(l):
            copy.wait_recv()

        def read(stage, v, q):
            if stage == 0:
                return state[l, v, q]
            return (one, two)[stage - 1][v, q]

        for stage in range(3):
            edge = [edges[l, stage, v] for v in range(V)]
            for q in range(1 + stage, 15 - stage):
                bg = [
                    jnp.broadcast_to(bgrows[q // 4, l, pl.ds(v * 4 + q % 4, 1), :], (K, COLS))
                    for v in range(V)
                ]
                here = [read(stage, v, q) for v in range(V)]
                rim = [pltpu.roll(edge[v], (124 - 8 * q) % COLS, 1) for v in range(V)]
                west = [jnp.where(lane == 0, rim[v], pltpu.roll(here[v], 1, 1)) for v in range(V)]
                east = [
                    jnp.where(lane == COLS - 1, rim[v], pltpu.roll(here[v], COLS - 1, 1))
                    for v in range(V)
                ]
                inc = increments(
                    [read(stage, v, q - 1) for v in range(V)], here,
                    [read(stage, v, q + 1) for v in range(V)], west, east, bg,
                )
                for v in range(V):
                    value = advance(stage, state[l, v, q], here[v], inc[v])
                    if stage == 0:
                        one[v, q] = value
                    elif stage == 1:
                        two[v, q] = value
                    else:
                        bred[l, v, q - 3] = value

        sums = [gacc[s] for s in range(SHIFTS)]
        for v in range(V):
            for rr in range(1, 9):
                tile = bred[l, v, rr]
                for s in range(SHIFTS):
                    other = tile if s == 0 else pltpu.roll(tile, K - s, 0)
                    sums[s] = sums[s] + tile * other
        for s in range(SHIFTS):
            gacc[s] = sums[s]

        for v in range(V):
            high, low = split(edges[l, 3, v])
            slots = jnp.where(
                (lane8 == 3) | (lane8 == 4), high,
                jnp.where((lane8 == 5) | (lane8 == 6), pltpu.roll(low, 2, 1), pltpu.roll(high, 4, 1)),
            )
            for rr in range(10):
                moved = pltpu.roll(slots, COLS - 8 * (rr + 3) - 3, 1)
                seams[v, rr] = jnp.where(lane < 6, moved, 0.0)
        high, low = split(bred[l].reshape(M_ROWS, COLS))
        lhs[:, 0:COLS] = high.astype(jnp.bfloat16)
        lhs[:, COLS : 2 * COLS] = low.astype(jnp.bfloat16)
        lhs[:, 2 * COLS : 3 * COLS] = high.astype(jnp.bfloat16)
        lhs[:, 3 * COLS :] = seams[...].reshape(M_ROWS, COLS).astype(jnp.bfloat16)

        def block(n, carry):
            columns = pl.ds(pl.multiple_of(n * WIDE, WIDE), WIDE)
            mixed = jnp.dot(lhs[...], weights[:, columns], preferred_element_type=jnp.float32)
            for i in range(WIDE // COLS):
                g = n * (WIDE // COLS) + i
                key = keys[g] - l * 16
                low = jnp.zeros((K, COLS), jnp.float32)
                high = low
                for v in range(V):
                    before = None
                    for rr in range(10):
                        at = (v * 10 + rr) * K
                        value = mixed[at : at + K, i * COLS : (i + 1) * COLS]
                        if before is not None:
                            high = jnp.where(before, value, high)
                        if rr < 9:
                            before = key == v * 64 + rr
                            low = jnp.where(before, value, low)
                proj[g] += row_w[g, 0] * low + row_w[g, 1] * high
            return carry

        lax.fori_loop(0, groups * COLS // WIDE, block, 0, unroll=8)
        return carry

    lax.fori_loop(0, L, level, 0)

    def weigh(g, sums):
        columns = pl.ds(pl.multiple_of(g * COLS, COLS), COLS)
        tile = proj[g]
        scaled = tile / err_ref[0:1, columns]
        return tuple(
            sums[s] + scaled * (tile if s == 0 else pltpu.roll(tile, K - s, 0))
            for s in range(SHIFTS)
        )

    zero = jnp.zeros((K, COLS), jnp.float32)
    normal = lax.fori_loop(0, groups, weigh, (zero,) * SHIFTS, unroll=8)
    mine = zero
    for s in range(SHIFTS):
        total = gacc[s] * (1.0 / cells_all) + normal[s] * (1.0 / obs_all)
        mine = jnp.where(lane == s, jnp.sum(total, axis=1, keepdims=True), mine)

    def all_sum(value, slots, me, peers, device, sends, recvs):
        part[...] = value
        slots[me] = value
        copies = [
            pltpu.make_async_remote_copy(
                src_ref=part, dst_ref=slots.at[me], send_sem=sends.at[d], recv_sem=recvs.at[d],
                device_id=device(peer), device_id_type=MESH,
            )
            for d, peer in enumerate(peers)
        ]
        for copy in copies:
            copy.start()
        for copy in copies:
            copy.wait()
        total = slots[0]
        for i in range(1, len(peers) + 1):
            total = total + slots[i]
        return total

    mine = all_sum(mine, sum_y, gy, y_peers, lambda p: (gx, p), ysend, yrecv)
    mine = all_sum(mine, sum_x, gx, x_peers, lambda p: (p, gy), xsend, xrecv)

    matrix = jnp.where(lane == sub + K, 1.0, 0.0)
    for s in range(K):
        if s < SHIFTS:
            diagonal = mine[:, s : s + 1]
        else:
            diagonal = pltpu.roll(mine, K - s, 0)[:, K - s : K - s + 1]
        matrix = jnp.where((lane < K) & (((lane - sub) & 7) == s), diagonal, matrix)
    scale = jnp.ones((K, COLS), jnp.float32)
    for j in range(K):
        pivot_row = jnp.broadcast_to(matrix[j : j + 1, :], (K, COLS))
        pivot = jnp.broadcast_to(pivot_row[:, j : j + 1], (K, COLS))
        column = jnp.broadcast_to(matrix[:, j : j + 1], (K, COLS))
        scale = jnp.where(sub == j, pivot, scale)
        matrix = jnp.where(sub > j, matrix - (column / pivot) * pivot_row, matrix)
    matrix = matrix / jnp.sqrt(scale)
    combo = [jnp.broadcast_to(matrix[:, K + j : K + j + 1], (K, COLS)) for j in range(K)]

    def mix(tile):
        terms = [combo[j] * jnp.broadcast_to(tile[j : j + 1, :], (K, COLS)) for j in range(K)]
        while len(terms) > 1:
            terms = [terms[i] + terms[i + 1] for i in range(0, len(terms), 2)]
        return terms[0]

    def write_obs(g, carry):
        columns = pl.ds(pl.multiple_of(g * COLS, COLS), COLS)
        obs_ref[:, columns] = mix(proj[g]) / jnp.sqrt(err_ref[0:1, columns])
        return carry

    lax.fori_loop(0, groups, write_obs, 0, unroll=4)
    obs_out = pltpu.make_async_copy(obs_ref, obs_hbm, store_sem.at[0])
    obs_out.start()

    def write(l, carry):
        for v in range(V):
            for r in range(ROWS):
                out_ref[pl.ds(v * L * ROWS + l * ROWS + r, K, stride=STRIDE), :] = mix(bred[l, v, r + 1])
        return carry

    lax.fori_loop(0, L, write, 0)

    out = pltpu.make_async_copy(out_ref, out_hbm, store_sem.at[1])
    out.start()
    for copy in near:
        copy.wait_send()
    for l in range(L):
        for copy in level_copies(l):
            copy.wait_send()
    obs_out.wait()
    out.wait()


def local(n_gx, n_gy, vectors, background, obs_site, obs_offset, obs_error):
    obs_dev = obs_site.shape[0]
    groups = obs_dev // COLS
    devices = n_gx * n_gy
    body = functools.partial(
        kernel, n_gx, n_gy, float(PLANES * ROWS * COLS * devices), float(obs_dev * devices)
    )
    f32 = jnp.float32
    hbm = pl.BlockSpec(memory_space=pltpu.HBM)
    analysis, obs = pl.pallas_call(
        body,
        out_shape=(
            jax.ShapeDtypeStruct((K * STRIDE, COLS), f32),
            jax.ShapeDtypeStruct((K, obs_dev), f32),
        ),
        in_specs=[hbm] * 5,
        out_specs=(hbm, hbm),
        scratch_shapes=[
            pltpu.VMEM((K * STRIDE, COLS), f32),
            pltpu.VMEM((K, obs_dev), f32),
            pltpu.SemaphoreType.DMA((2,)),
            pltpu.VMEM((K * STRIDE, COLS), f32),
            pltpu.VMEM((V * L * ROWS, COLS), f32),
            pltpu.VMEM((groups, COLS), jnp.int32),
            pltpu.VMEM((2, obs_dev), f32),
            pltpu.VMEM((1, obs_dev), f32),
            pltpu.SemaphoreType.DMA((5,)),
            pltpu.VMEM((4 * COLS, obs_dev), jnp.bfloat16),
            pltpu.VMEM((M_ROWS, 4 * COLS), jnp.bfloat16),
            pltpu.VMEM((V, 10, K, COLS), f32),
            pltpu.VMEM((groups, K, COLS), jnp.int32),
            pltpu.VMEM((groups, 2, K, COLS), f32),
            pltpu.VMEM((L, V, 16, K, COLS), f32),
            pltpu.VMEM((V, 16, K, COLS), f32),
            pltpu.VMEM((V, 16, K, COLS), f32),
            pltpu.VMEM((L, V, 10, K, COLS), f32),
            pltpu.VMEM((4, L, 16, COLS), f32),
            pltpu.VMEM((3, 4, V + 1, K, COLS), f32),
            pltpu.VMEM((L, 4, V, K, COLS), f32),
            pltpu.VMEM((groups, K, COLS), f32),
            pltpu.VMEM((SHIFTS, K, COLS), f32),
            pltpu.VMEM((n_gy, K, COLS), f32),
            pltpu.VMEM((n_gx, K, COLS), f32),
            pltpu.VMEM((K, COLS), f32),
            pltpu.SemaphoreType.DMA((N_COPIES,)),
            pltpu.SemaphoreType.DMA((N_COPIES,)),
            pltpu.SemaphoreType.DMA((n_gy - 1,)),
            pltpu.SemaphoreType.DMA((n_gy - 1,)),
            pltpu.SemaphoreType.DMA((n_gx - 1,)),
            pltpu.SemaphoreType.DMA((n_gx - 1,)),
        ],
        compiler_params=pltpu.CompilerParams(
            collective_id=0, has_side_effects=True, vmem_limit_bytes=63 * 1024 * 1024
        ),
    )(
        vectors.reshape(K * STRIDE, COLS),
        background.reshape(V * L * ROWS, COLS),
        obs_site.reshape(groups, COLS),
        obs_offset,
        obs_error.reshape(1, obs_dev),
    )
    return analysis.reshape(vectors.shape), obs


def solution(mesh):
    placed = (
        P(None, None, None, "gx", "gy"),
        P(None, None, "gx", "gy"),
        P(("gx", "gy")),
        P(None, ("gx", "gy")),
        P(("gx", "gy")),
    )
    return jax.shard_map(
        functools.partial(local, mesh.shape["gx"], mesh.shape["gy"]),
        mesh=mesh,
        in_specs=placed,
        out_specs=(P(None, None, None, "gx", "gy"), P(None, ("gx", "gy"))),
        check_vma=False,
    )
```

```python
import functools

import jax
import jax.numpy as jnp
from jax import lax
from jax.experimental import pallas as pl
from jax.experimental.pallas import tpu as pltpu
from jax.sharding import PartitionSpec as P

K = 8
V = 3
L = 4
ROWS = 8
COLS = 128
PLANES = V * L
STRIDE = PLANES * ROWS
STEP = 0.35
MESH = pl.DeviceIdType.MESH
SHIFTS = 5
N_EDGE = 8
M_ROWS = V * 10 * K
WIDE = 256
N_COPIES = N_EDGE + 2 + 2 * L


def increments(below, here, above, west, east, bg):
    wx, wy, va = bg
    dx = [above[i] - below[i] for i in range(V)]
    dy = [east[i] - west[i] for i in range(V)]
    half = 0.5 * STEP
    hx, hy, sv = half * wx, half * wy, STEP * va
    inc_e = sv * here[1] - (hx * dx[0] + hy * dy[0]) - half * dx[2]
    inc_n = -(sv * here[0]) - (hx * dx[1] + hy * dy[1]) - half * dy[2]
    inc_h = -(hx * dx[2] + hy * dy[2]) - half * (dx[0] + dy[1])
    return inc_e, inc_n, inc_h


def advance(stage, start, here, inc):
    if stage == 0:
        return here + inc
    if stage == 1:
        return 0.75 * start + 0.25 * (here + inc)
    return (1.0 / 3.0) * start + (2.0 / 3.0) * (here + inc)


def split(value):
    high = value.astype(jnp.bfloat16).astype(jnp.float32)
    return high, value - high


def kernel(
    n_gx, n_gy, cells_all, obs_all,
    vec_hbm, bg_hbm, site_hbm, off_hbm, err_hbm,
    bred_hbm, proj_hbm, matrix_ref, store_sem,
    vec_ref, bg_ref, site_ref, off_ref, err_ref, load_sem,
    weights, lhs, seams, keys, row_w,
    state, one, two, bred, bgrows, strips, edges, proj, gacc, sum_y, sum_x, part,
    send_sem, recv_sem, ysend, yrecv, xsend, xrecv,
):
    groups = proj.shape[0]
    gx = lax.axis_index("gx")
    gy = lax.axis_index("gy")
    up, dn = lax.rem(gx + n_gx - 1, n_gx), lax.rem(gx + 1, n_gx)
    lf, rt = lax.rem(gy + n_gy - 1, n_gy), lax.rem(gy + 1, n_gy)
    x_peers = [lax.rem(gx + d, n_gx) for d in range(1, n_gx)]
    y_peers = [lax.rem(gy + d, n_gy) for d in range(1, n_gy)]
    lane = lax.broadcasted_iota(jnp.int32, (K, COLS), 1)
    sub = lax.broadcasted_iota(jnp.int32, (K, COLS), 0)
    lane8 = lane & 7

    loads = [
        pltpu.make_async_copy(src, dst, load_sem.at[i])
        for i, (src, dst) in enumerate(
            [(bg_hbm, bg_ref), (vec_hbm, vec_ref), (site_hbm, site_ref),
             (off_hbm, off_ref), (err_hbm, err_ref)]
        )
    ]
    for copy in loads:
        copy.start()

    barrier = pltpu.get_barrier_semaphore()
    greeted = [(a, b) for a in (up, dn) for b in (lf, rt)]
    direct = sum_x.shape[0] == n_gx * n_gy
    if direct:
        peers = [
            (lax.rem(gx + i, n_gx), lax.rem(gy + j, n_gy))
            for i in range(n_gx) for j in range(n_gy) if i + j > 0
        ]
        greeted = peers
    else:
        greeted += [(a, gy) for a in x_peers] + [(gx, b) for b in y_peers]
    for peer in greeted:
        pl.semaphore_signal(barrier, inc=1, device_id=peer, device_id_type=MESH)

    loads[0].wait()
    loads[1].wait()
    packed = [[jnp.zeros((K, COLS), jnp.float32) for _ in range(V + 1)] for _ in range(2)]
    for l in range(L):
        for r in range(ROWS):
            h, base = r // 4, l * 32 + (r % 4) * 8
            put = (lane >> 3) == base // 8
            for v in range(V):
                tile = vec_ref[pl.ds((v * L + l) * ROWS + r, K, stride=STRIDE), :]
                state[l, v, 4 + r] = tile
                packed[h][v] = jnp.where(put, pltpu.roll(tile, (base + 4) % COLS, 1), packed[h][v])
            rows = [
                jnp.broadcast_to(bg_ref[pl.ds((v * L + l) * ROWS + r, 1), :], (K, COLS))
                for v in range(V)
            ]
            tile = jnp.where(sub == 0, rows[0], jnp.where(sub == 1, rows[1], rows[2]))
            packed[h][V] = jnp.where(put, pltpu.roll(tile, (base + 4) % COLS, 1), packed[h][V])
        for h in range(2):
            for v in range(V):
                bgrows[1 + h, l, pl.ds(v * 4, 4), :] = bg_ref[pl.ds((v * L + l) * ROWS + h * 4, 4), :]
            bgrows[1 + h, l, pl.ds(12, 4), :] = jnp.zeros((4, COLS), jnp.float32)
    for h in range(2):
        for v in range(V + 1):
            strips[1, 1 + h, v] = packed[h][v]

    pl.semaphore_wait(barrier, len(greeted))

    def remote(src, dst, index, peer):
        return pltpu.make_async_remote_copy(
            src_ref=src, dst_ref=dst, send_sem=send_sem.at[index], recv_sem=recv_sem.at[index],
            device_id=peer, device_id_type=MESH,
        )

    both = pl.ds(1, 2)
    near = [
        remote(strips.at[1, 1], strips.at[1, 3], 0, (up, gy)),
        remote(strips.at[1, 2], strips.at[1, 0], 1, (dn, gy)),
        remote(strips.at[1, 1], strips.at[2, 3], 2, (up, lf)),
        remote(strips.at[1, 1], strips.at[0, 3], 3, (up, rt)),
        remote(strips.at[1, 2], strips.at[2, 0], 4, (dn, lf)),
        remote(strips.at[1, 2], strips.at[0, 0], 5, (dn, rt)),
        remote(strips.at[1, both], strips.at[2, both], 6, (gx, lf)),
        remote(strips.at[1, both], strips.at[0, both], 7, (gx, rt)),
        remote(bgrows.at[1], bgrows.at[3], 8, (up, gy)),
        remote(bgrows.at[2], bgrows.at[0], 9, (dn, gy)),
    ]

    def level_copies(l):
        return (
            remote(state.at[l, :, pl.ds(4, 4)], state.at[l, :, pl.ds(12, 4)], 10 + 2 * l, (up, gy)),
            remote(state.at[l, :, pl.ds(8, 4)], state.at[l, :, pl.ds(0, 4)], 11 + 2 * l, (dn, gy)),
        )

    for copy in near:
        copy.start()
    for l in range(L):
        for copy in level_copies(l):
            copy.start()

    gacc[...] = jnp.zeros_like(gacc)
    proj[...] = jnp.zeros_like(proj)
    for copy in loads[2:]:
        copy.wait()

    cell = lax.broadcasted_iota(jnp.int32, (COLS, COLS), 0)
    slot = lax.broadcasted_iota(jnp.int32, (16, COLS), 0)
    weights[pl.ds(3 * COLS, COLS), :] = jnp.zeros((COLS, groups * COLS), jnp.bfloat16)

    def weigh_columns(g, carry):
        columns = pl.ds(pl.multiple_of(g * COLS, COLS), COLS)
        site = site_ref[pl.ds(g, 1), :]
        a, b = off_ref[0:1, columns], off_ref[1:2, columns]
        row, col = (site >> 7) & 7, site & 127
        abs_a, abs_b = jnp.abs(a), jnp.abs(b)
        row0 = jnp.where(a < 0.0, row - 1, row)
        col0 = jnp.where(b < 0.0, col - 1, col)
        keys[g] = jnp.broadcast_to((site >> 10) * 16 + row0 + 1, (K, COLS))
        row_w[g, 0] = jnp.broadcast_to(jnp.where(a < 0.0, abs_a, 1.0 - abs_a), (K, COLS))
        row_w[g, 1] = jnp.broadcast_to(jnp.where(a < 0.0, 1.0 - abs_a, abs_a), (K, COLS))
        w0 = jnp.where(b < 0.0, abs_b, 1.0 - abs_b)
        w1 = jnp.where(b < 0.0, 1.0 - abs_b, abs_b)
        high, low = split(
            jnp.where(cell == col0, w0, 0.0) + jnp.where(cell == col0 + 1, w1, 0.0)
        )
        weights[pl.ds(0, COLS), columns] = high.astype(jnp.bfloat16)
        weights[pl.ds(COLS, COLS), columns] = high.astype(jnp.bfloat16)
        weights[pl.ds(2 * COLS, COLS), columns] = low.astype(jnp.bfloat16)
        at_left = jnp.where(col0 < 0, w0, 0.0)
        at_right = jnp.where(col0 >= COLS - 1, w1, 0.0)
        high, low = split(jnp.where((slot & 1) == 0, at_right, at_left))
        seam = jnp.where(slot < 4, high, jnp.where(slot < 6, low, 0.0))
        weights[pl.ds(3 * COLS, 16), columns] = seam.astype(jnp.bfloat16)
        return carry

    lax.fori_loop(0, groups, weigh_columns, 0)
    for copy in near:
        copy.wait_recv()

    for l in range(L):
        whole = []
        for side in range(3):
            fields = []
            for v in range(V + 1):
                tile = jnp.zeros((K, COLS), jnp.float32)
                for seg in range(4):
                    moved = pltpu.roll(strips[side, seg, v], (seg + 4 - l) * 32 % COLS, 1)
                    tile = jnp.where((lane >> 5) == seg, moved, tile)
                fields.append(tile)
            whole.append(fields)
        inner = lane8 < 4
        sides = []
        for a, b in ((0, 1), (1, 2)):
            fields = [jnp.where(inner, whole[a][v], whole[b][v]) for v in range(V + 1)]
            bg = [jnp.broadcast_to(fields[V][i : i + 1, :], (K, COLS)) for i in range(3)]
            start = fields[:V]
            here = start
            history = [start]
            for stage in range(3):
                inc = increments(
                    [pltpu.roll(f, 8, 1) for f in here], here,
                    [pltpu.roll(f, COLS - 8, 1) for f in here],
                    [pltpu.roll(f, 1, 1) for f in here],
                    [pltpu.roll(f, COLS - 1, 1) for f in here], bg,
                )
                here = [advance(stage, start[v], here[v], inc[v]) for v in range(V)]
                history.append(here)
            sides.append(history)
        for stage in range(4):
            for v in range(V):
                left, right = sides[0][stage][v], sides[1][stage][v]
                edges[l, stage, v] = jnp.where(
                    lane8 == 4, pltpu.roll(left, 1, 1), pltpu.roll(right, COLS - 1, 1)
                )

    def stored(l):
        return pltpu.make_async_copy(
            bred.at[l, :, pl.ds(1, ROWS)], bred_hbm.at[l], store_sem.at[l]
        )

    def level(l, carry):
        for copy in level_copies(l):
            copy.wait_recv()

        def read(stage, v, q):
            if stage == 0:
                return state[l, v, q]
            return (one, two)[stage - 1][v, q]

        for stage in range(3):
            edge = [edges[l, stage, v] for v in range(V)]
            for q in range(1 + stage, 15 - stage):
                bg = [
                    jnp.broadcast_to(bgrows[q // 4, l, pl.ds(v * 4 + q % 4, 1), :], (K, COLS))
                    for v in range(V)
                ]
                here = [read(stage, v, q) for v in range(V)]
                rim = [pltpu.roll(edge[v], (124 - 8 * q) % COLS, 1) for v in range(V)]
                west = [jnp.where(lane == 0, rim[v], pltpu.roll(here[v], 1, 1)) for v in range(V)]
                east = [
                    jnp.where(lane == COLS - 1, rim[v], pltpu.roll(here[v], COLS - 1, 1))
                    for v in range(V)
                ]
                inc = increments(
                    [read(stage, v, q - 1) for v in range(V)], here,
                    [read(stage, v, q + 1) for v in range(V)], west, east, bg,
                )
                for v in range(V):
                    value = advance(stage, state[l, v, q], here[v], inc[v])
                    if stage == 0:
                        one[v, q] = value
                    elif stage == 1:
                        two[v, q] = value
                    else:
                        bred[l, v, q - 3] = value

        sums = [gacc[s] for s in range(SHIFTS)]
        for v in range(V):
            for rr in range(1, 9):
                tile = bred[l, v, rr]
                for s in range(SHIFTS):
                    other = tile if s == 0 else pltpu.roll(tile, K - s, 0)
                    sums[s] = sums[s] + tile * other
        for s in range(SHIFTS):
            gacc[s] = sums[s]

        for v in range(V):
            high, low = split(edges[l, 3, v])
            slots = jnp.where(
                (lane8 == 3) | (lane8 == 4), high,
                jnp.where((lane8 == 5) | (lane8 == 6), pltpu.roll(low, 2, 1), pltpu.roll(high, 4, 1)),
            )
            for rr in range(10):
                moved = pltpu.roll(slots, COLS - 8 * (rr + 3) - 3, 1)
                seams[v, rr] = jnp.where(lane < 6, moved, 0.0)
        high, low = split(bred[l].reshape(M_ROWS, COLS))
        lhs[:, 0:COLS] = high.astype(jnp.bfloat16)
        lhs[:, COLS : 2 * COLS] = low.astype(jnp.bfloat16)
        lhs[:, 2 * COLS : 3 * COLS] = high.astype(jnp.bfloat16)
        lhs[:, 3 * COLS :] = seams[...].reshape(M_ROWS, COLS).astype(jnp.bfloat16)

        def block(n, carry):
            columns = pl.ds(pl.multiple_of(n * WIDE, WIDE), WIDE)
            mixed = jnp.dot(lhs[...], weights[:, columns], preferred_element_type=jnp.float32)
            for i in range(WIDE // COLS):
                g = n * (WIDE // COLS) + i
                key = keys[g] - l * 16
                low = jnp.zeros((K, COLS), jnp.float32)
                high = low
                for v in range(V):
                    before = None
                    for rr in range(10):
                        at = (v * 10 + rr) * K
                        value = mixed[at : at + K, i * COLS : (i + 1) * COLS]
                        if before is not None:
                            high = jnp.where(before, value, high)
                        if rr < 9:
                            before = key == v * 64 + rr
                            low = jnp.where(before, value, low)
                proj[g] += row_w[g, 0] * low + row_w[g, 1] * high
            return carry

        stored(l).start()
        lax.fori_loop(0, groups * COLS // WIDE, block, 0, unroll=8)
        return carry

    lax.fori_loop(0, L, level, 0)
    proj_out = pltpu.make_async_copy(proj, proj_hbm, store_sem.at[L])
    proj_out.start()

    def weigh(g, sums):
        columns = pl.ds(pl.multiple_of(g * COLS, COLS), COLS)
        tile = proj[g]
        scaled = tile / err_ref[0:1, columns]
        return tuple(
            sums[s] + scaled * (tile if s == 0 else pltpu.roll(tile, K - s, 0))
            for s in range(SHIFTS)
        )

    zero = jnp.zeros((K, COLS), jnp.float32)
    normal = lax.fori_loop(0, groups, weigh, (zero,) * SHIFTS, unroll=8)
    mine = zero
    for s in range(SHIFTS):
        total = gacc[s] * (1.0 / cells_all) + normal[s] * (1.0 / obs_all)
        mine = jnp.where(lane == s, jnp.sum(total, axis=1, keepdims=True), mine)

    def all_sum(value, slots, me, peers, device, sends, recvs):
        part[...] = value
        slots[me] = value
        copies = [
            pltpu.make_async_remote_copy(
                src_ref=part, dst_ref=slots.at[me], send_sem=sends.at[d], recv_sem=recvs.at[d],
                device_id=device(peer), device_id_type=MESH,
            )
            for d, peer in enumerate(peers)
        ]
        for copy in copies:
            copy.start()
        for copy in copies:
            copy.wait()
        terms = [slots[i] for i in range(len(peers) + 1)]
        while len(terms) > 1:
            terms = [sum(terms[i : i + 2][1:], terms[i]) for i in range(0, len(terms), 2)]
        return terms[0]

    if direct:
        mine = all_sum(mine, sum_x, gx * n_gy + gy, peers, lambda p: p, xsend, xrecv)
    else:
        mine = all_sum(mine, sum_y, gy, y_peers, lambda p: (gx, p), ysend, yrecv)
        mine = all_sum(mine, sum_x, gx, x_peers, lambda p: (p, gy), xsend, xrecv)

    matrix = jnp.where(lane == sub + K, 1.0, 0.0)
    for s in range(K):
        if s < SHIFTS:
            diagonal = mine[:, s : s + 1]
        else:
            diagonal = pltpu.roll(mine, K - s, 0)[:, K - s : K - s + 1]
        matrix = jnp.where((lane < K) & (((lane - sub) & 7) == s), diagonal, matrix)
    scale = jnp.ones((K, COLS), jnp.float32)
    for j in range(K):
        pivot_row = jnp.broadcast_to(matrix[j : j + 1, :], (K, COLS))
        pivot = jnp.broadcast_to(pivot_row[:, j : j + 1], (K, COLS))
        column = jnp.broadcast_to(matrix[:, j : j + 1], (K, COLS))
        scale = jnp.where(sub == j, pivot, scale)
        matrix = jnp.where(sub > j, matrix - (column / pivot) * pivot_row, matrix)
    matrix = matrix / jnp.sqrt(scale)
    matrix_ref[...] = matrix
    for copy in near:
        copy.wait_send()
    for l in range(L):
        for copy in level_copies(l):
            copy.wait_send()
        stored(l).wait()
    proj_out.wait()


def mix_kernel(
    bred_hbm, proj_hbm, matrix_hbm, err_hbm, out_hbm, obs_hbm,
    bred, proj, matrix_ref, err_ref, out, obs, load_sem, out_sem,
):
    groups = proj.shape[0]
    loads = [
        pltpu.make_async_copy(src, dst, load_sem.at[i])
        for i, (src, dst) in enumerate([(matrix_hbm, matrix_ref), (err_hbm, err_ref), (proj_hbm, proj)])
    ]
    loads += [
        pltpu.make_async_copy(bred_hbm.at[:, v], bred.at[:, v], load_sem.at[3 + v]) for v in range(V)
    ]
    for copy in loads:
        copy.start()
    for copy in loads[:3]:
        copy.wait()
    matrix = matrix_ref[...]
    combo = [jnp.broadcast_to(matrix[:, K + j : K + j + 1], (K, COLS)) for j in range(K)]

    def mix(tile):
        terms = [combo[j] * jnp.broadcast_to(tile[j : j + 1, :], (K, COLS)) for j in range(K)]
        while len(terms) > 1:
            terms = [terms[i] + terms[i + 1] for i in range(0, len(terms), 2)]
        return terms[0]

    def write_obs(g, carry):
        columns = pl.ds(pl.multiple_of(g * COLS, COLS), COLS)
        obs[:, columns] = mix(proj[g]) / jnp.sqrt(err_ref[0:1, columns])
        return carry

    lax.fori_loop(0, groups, write_obs, 0, unroll=8)
    stores = [pltpu.make_async_copy(obs, obs_hbm, out_sem.at[0])]
    stores[0].start()
    part = L * ROWS
    for v in range(V):
        loads[3 + v].wait()
        for l in range(L):
            for r in range(ROWS):
                out[pl.ds(v * K * part + l * ROWS + r, K, stride=part), :] = mix(bred[l, v, r])
        for k in range(K):
            copy = pltpu.make_async_copy(
                out.at[pl.ds((v * K + k) * part, part)],
                out_hbm.at[pl.ds((k * V + v) * part, part)],
                out_sem.at[1 + v * K + k],
            )
            copy.start()
            stores.append(copy)
    for copy in stores:
        copy.wait()


def local(n_gx, n_gy, vectors, background, obs_site, obs_offset, obs_error):
    obs_dev = obs_site.shape[0]
    groups = obs_dev // COLS
    devices = n_gx * n_gy
    body = functools.partial(
        kernel, n_gx, n_gy, float(PLANES * ROWS * COLS * devices), float(obs_dev * devices)
    )
    f32 = jnp.float32
    slots = devices if devices <= 64 else n_gx
    vmem = pl.BlockSpec(memory_space=pltpu.VMEM)
    hbm = pl.BlockSpec(memory_space=pltpu.HBM)
    error = obs_error.reshape(1, obs_dev)
    bred, proj, matrix = pl.pallas_call(
        body,
        out_shape=(
            jax.ShapeDtypeStruct((L, V, ROWS, K, COLS), f32),
            jax.ShapeDtypeStruct((groups, K, COLS), f32),
            jax.ShapeDtypeStruct((K, COLS), f32),
        ),
        in_specs=[hbm] * 5,
        out_specs=(hbm, hbm, vmem),
        scratch_shapes=[
            pltpu.SemaphoreType.DMA((L + 1,)),
            pltpu.VMEM((K * STRIDE, COLS), f32),
            pltpu.VMEM((V * L * ROWS, COLS), f32),
            pltpu.VMEM((groups, COLS), jnp.int32),
            pltpu.VMEM((2, obs_dev), f32),
            pltpu.VMEM((1, obs_dev), f32),
            pltpu.SemaphoreType.DMA((5,)),
            pltpu.VMEM((4 * COLS, obs_dev), jnp.bfloat16),
            pltpu.VMEM((M_ROWS, 4 * COLS), jnp.bfloat16),
            pltpu.VMEM((V, 10, K, COLS), f32),
            pltpu.VMEM((groups, K, COLS), jnp.int32),
            pltpu.VMEM((groups, 2, K, COLS), f32),
            pltpu.VMEM((L, V, 16, K, COLS), f32),
            pltpu.VMEM((V, 16, K, COLS), f32),
            pltpu.VMEM((V, 16, K, COLS), f32),
            pltpu.VMEM((L, V, 10, K, COLS), f32),
            pltpu.VMEM((4, L, 16, COLS), f32),
            pltpu.VMEM((3, 4, V + 1, K, COLS), f32),
            pltpu.VMEM((L, 4, V, K, COLS), f32),
            pltpu.VMEM((groups, K, COLS), f32),
            pltpu.VMEM((SHIFTS, K, COLS), f32),
            pltpu.VMEM((n_gy, K, COLS), f32),
            pltpu.VMEM((slots, K, COLS), f32),
            pltpu.VMEM((K, COLS), f32),
            pltpu.SemaphoreType.DMA((N_COPIES,)),
            pltpu.SemaphoreType.DMA((N_COPIES,)),
            pltpu.SemaphoreType.DMA((n_gy - 1,)),
            pltpu.SemaphoreType.DMA((n_gy - 1,)),
            pltpu.SemaphoreType.DMA((slots - 1,)),
            pltpu.SemaphoreType.DMA((slots - 1,)),
        ],
        compiler_params=pltpu.CompilerParams(
            collective_id=0, has_side_effects=True, vmem_limit_bytes=63 * 1024 * 1024
        ),
    )(
        vectors.reshape(K * STRIDE, COLS),
        background.reshape(V * L * ROWS, COLS),
        obs_site.reshape(groups, COLS),
        obs_offset,
        error,
    )
    analysis, obs = pl.pallas_call(
        mix_kernel,
        out_shape=(
            jax.ShapeDtypeStruct((K * STRIDE, COLS), f32),
            jax.ShapeDtypeStruct((K, obs_dev), f32),
        ),
        in_specs=[hbm] * 4,
        out_specs=(hbm, hbm),
        scratch_shapes=[
            pltpu.VMEM((L, V, ROWS, K, COLS), f32),
            pltpu.VMEM((groups, K, COLS), f32),
            pltpu.VMEM((K, COLS), f32),
            pltpu.VMEM((1, obs_dev), f32),
            pltpu.VMEM((K * STRIDE, COLS), f32),
            pltpu.VMEM((K, obs_dev), f32),
            pltpu.SemaphoreType.DMA((3 + V,)),
            pltpu.SemaphoreType.DMA((1 + V * K,)),
        ],
        compiler_params=pltpu.CompilerParams(vmem_limit_bytes=63 * 1024 * 1024),
    )(bred, proj, matrix, error)
    return analysis.reshape(vectors.shape), obs


def solution(mesh):
    placed = (
        P(None, None, None, "gx", "gy"),
        P(None, None, "gx", "gy"),
        P(("gx", "gy")),
        P(None, ("gx", "gy")),
        P(("gx", "gy")),
    )
    return jax.shard_map(
        functools.partial(local, mesh.shape["gx"], mesh.shape["gy"]),
        mesh=mesh,
        in_specs=placed,
        out_specs=(P(None, None, None, "gx", "gy"), P(None, ("gx", "gy"))),
        check_vma=False,
    )
```

```python
import functools

import jax
import jax.numpy as jnp
from jax import lax
from jax.experimental import pallas as pl
from jax.experimental.pallas import tpu as pltpu
from jax.sharding import PartitionSpec as P

K = 8
V = 3
L = 4
ROWS = 8
COLS = 128
PLANES = V * L
STRIDE = PLANES * ROWS
STEP = 0.35
MESH = pl.DeviceIdType.MESH
SHIFTS = 5
N_EDGE = 8
M_ROWS = V * 10 * K
WIDE = 256
PAIR = 2
N_COPIES = N_EDGE + 2 + 2 * L


def increments(below, here, above, west, east, bg):
    wx, wy, va = bg
    dx = [above[i] - below[i] for i in range(V)]
    dy = [east[i] - west[i] for i in range(V)]
    half = 0.5 * STEP
    hx, hy, sv = half * wx, half * wy, STEP * va
    inc_e = sv * here[1] - (hx * dx[0] + hy * dy[0]) - half * dx[2]
    inc_n = -(sv * here[0]) - (hx * dx[1] + hy * dy[1]) - half * dy[2]
    inc_h = -(hx * dx[2] + hy * dy[2]) - half * (dx[0] + dy[1])
    return inc_e, inc_n, inc_h


def advance(stage, start, here, inc):
    if stage == 0:
        return here + inc
    if stage == 1:
        return 0.75 * start + 0.25 * (here + inc)
    return (1.0 / 3.0) * start + (2.0 / 3.0) * (here + inc)


def split(value):
    high = value.astype(jnp.bfloat16).astype(jnp.float32)
    return high, value - high


def kernel(
    n_gx, n_gy, cells_all, obs_all,
    vec_hbm, bg_hbm, site_hbm, off_hbm, err_hbm,
    bred_hbm, proj_hbm, matrix_ref, store_sem,
    vec_ref, bg_ref, site_ref, off_ref, err_ref, load_sem,
    weights, lhs, seams, keys, row_w,
    state, one, two, bred, bgrows, strips, edges, proj, gacc, sum_y, sum_x, part,
    send_sem, recv_sem, ysend, yrecv, xsend, xrecv,
):
    groups = proj.shape[0]
    gx = lax.axis_index("gx")
    gy = lax.axis_index("gy")
    up, dn = lax.rem(gx + n_gx - 1, n_gx), lax.rem(gx + 1, n_gx)
    lf, rt = lax.rem(gy + n_gy - 1, n_gy), lax.rem(gy + 1, n_gy)
    x_peers = [lax.rem(gx + d, n_gx) for d in range(1, n_gx)]
    y_peers = [lax.rem(gy + d, n_gy) for d in range(1, n_gy)]
    lane = lax.broadcasted_iota(jnp.int32, (K, COLS), 1)
    sub = lax.broadcasted_iota(jnp.int32, (K, COLS), 0)
    lane8 = lane & 7

    loads = [
        pltpu.make_async_copy(src, dst, load_sem.at[i])
        for i, (src, dst) in enumerate(
            [(bg_hbm, bg_ref), (vec_hbm, vec_ref), (site_hbm, site_ref),
             (off_hbm, off_ref), (err_hbm, err_ref)]
        )
    ]
    for copy in loads:
        copy.start()

    barrier = pltpu.get_barrier_semaphore()
    greeted = [(a, b) for a in (up, dn) for b in (lf, rt)]
    direct = sum_x.shape[0] == n_gx * n_gy
    if direct:
        peers = [
            (lax.rem(gx + i, n_gx), lax.rem(gy + j, n_gy))
            for i in range(n_gx) for j in range(n_gy) if i + j > 0
        ]
        greeted = peers
    else:
        greeted += [(a, gy) for a in x_peers] + [(gx, b) for b in y_peers]
    for peer in greeted:
        pl.semaphore_signal(barrier, inc=1, device_id=peer, device_id_type=MESH)

    loads[0].wait()
    loads[1].wait()
    packed = [[jnp.zeros((K, COLS), jnp.float32) for _ in range(V + 1)] for _ in range(2)]
    for l in range(L):
        for r in range(ROWS):
            h, base = r // 4, l * 32 + (r % 4) * 8
            put = (lane >> 3) == base // 8
            for v in range(V):
                tile = vec_ref[pl.ds((v * L + l) * ROWS + r, K, stride=STRIDE), :]
                state[l, v, 4 + r] = tile
                packed[h][v] = jnp.where(put, pltpu.roll(tile, (base + 4) % COLS, 1), packed[h][v])
            rows = [
                jnp.broadcast_to(bg_ref[pl.ds((v * L + l) * ROWS + r, 1), :], (K, COLS))
                for v in range(V)
            ]
            tile = jnp.where(sub == 0, rows[0], jnp.where(sub == 1, rows[1], rows[2]))
            packed[h][V] = jnp.where(put, pltpu.roll(tile, (base + 4) % COLS, 1), packed[h][V])
        for h in range(2):
            for v in range(V):
                bgrows[1 + h, l, pl.ds(v * 4, 4), :] = bg_ref[pl.ds((v * L + l) * ROWS + h * 4, 4), :]
            bgrows[1 + h, l, pl.ds(12, 4), :] = jnp.zeros((4, COLS), jnp.float32)
    for h in range(2):
        for v in range(V + 1):
            strips[1, 1 + h, v] = packed[h][v]

    pl.semaphore_wait(barrier, len(greeted))

    def remote(src, dst, index, peer):
        return pltpu.make_async_remote_copy(
            src_ref=src, dst_ref=dst, send_sem=send_sem.at[index], recv_sem=recv_sem.at[index],
            device_id=peer, device_id_type=MESH,
        )

    both = pl.ds(1, 2)
    near = [
        remote(strips.at[1, 1], strips.at[1, 3], 0, (up, gy)),
        remote(strips.at[1, 2], strips.at[1, 0], 1, (dn, gy)),
        remote(strips.at[1, 1], strips.at[2, 3], 2, (up, lf)),
        remote(strips.at[1, 1], strips.at[0, 3], 3, (up, rt)),
        remote(strips.at[1, 2], strips.at[2, 0], 4, (dn, lf)),
        remote(strips.at[1, 2], strips.at[0, 0], 5, (dn, rt)),
        remote(strips.at[1, both], strips.at[2, both], 6, (gx, lf)),
        remote(strips.at[1, both], strips.at[0, both], 7, (gx, rt)),
        remote(bgrows.at[1], bgrows.at[3], 8, (up, gy)),
        remote(bgrows.at[2], bgrows.at[0], 9, (dn, gy)),
    ]

    def level_copies(l):
        return (
            remote(state.at[l, :, pl.ds(4, 4)], state.at[l, :, pl.ds(12, 4)], 10 + 2 * l, (up, gy)),
            remote(state.at[l, :, pl.ds(8, 4)], state.at[l, :, pl.ds(0, 4)], 11 + 2 * l, (dn, gy)),
        )

    for copy in near:
        copy.start()
    for l in range(L):
        for copy in level_copies(l):
            copy.start()

    gacc[...] = jnp.zeros_like(gacc)
    proj[...] = jnp.zeros_like(proj)
    for copy in loads[2:]:
        copy.wait()

    cell = lax.broadcasted_iota(jnp.int32, (COLS, COLS), 0)
    slot = lax.broadcasted_iota(jnp.int32, (16, COLS), 0)
    weights[pl.ds(3 * COLS, COLS), :] = jnp.zeros((COLS, groups * COLS), jnp.bfloat16)

    def weigh_columns(g, carry):
        columns = pl.ds(pl.multiple_of(g * COLS, COLS), COLS)
        site = site_ref[pl.ds(g, 1), :]
        a, b = off_ref[0:1, columns], off_ref[1:2, columns]
        row, col = (site >> 7) & 7, site & 127
        abs_a, abs_b = jnp.abs(a), jnp.abs(b)
        row0 = jnp.where(a < 0.0, row - 1, row)
        col0 = jnp.where(b < 0.0, col - 1, col)
        keys[g] = jnp.broadcast_to((site >> 10) * 16 + row0 + 1, (K, COLS))
        row_w[g, 0] = jnp.broadcast_to(jnp.where(a < 0.0, abs_a, 1.0 - abs_a), (K, COLS))
        row_w[g, 1] = jnp.broadcast_to(jnp.where(a < 0.0, 1.0 - abs_a, abs_a), (K, COLS))
        w0 = jnp.where(b < 0.0, abs_b, 1.0 - abs_b)
        w1 = jnp.where(b < 0.0, 1.0 - abs_b, abs_b)
        high, low = split(
            jnp.where(cell == col0, w0, 0.0) + jnp.where(cell == col0 + 1, w1, 0.0)
        )
        weights[pl.ds(0, COLS), columns] = high.astype(jnp.bfloat16)
        weights[pl.ds(COLS, COLS), columns] = high.astype(jnp.bfloat16)
        weights[pl.ds(2 * COLS, COLS), columns] = low.astype(jnp.bfloat16)
        at_left = jnp.where(col0 < 0, w0, 0.0)
        at_right = jnp.where(col0 >= COLS - 1, w1, 0.0)
        high, low = split(jnp.where((slot & 1) == 0, at_right, at_left))
        seam = jnp.where(slot < 4, high, jnp.where(slot < 6, low, 0.0))
        weights[pl.ds(3 * COLS, 16), columns] = seam.astype(jnp.bfloat16)
        return carry

    lax.fori_loop(0, groups, weigh_columns, 0)
    for copy in near:
        copy.wait_recv()

    for l in range(L):
        whole = []
        for side in range(3):
            fields = []
            for v in range(V + 1):
                tile = jnp.zeros((K, COLS), jnp.float32)
                for seg in range(4):
                    moved = pltpu.roll(strips[side, seg, v], (seg + 4 - l) * 32 % COLS, 1)
                    tile = jnp.where((lane >> 5) == seg, moved, tile)
                fields.append(tile)
            whole.append(fields)
        inner = lane8 < 4
        sides = []
        for a, b in ((0, 1), (1, 2)):
            fields = [jnp.where(inner, whole[a][v], whole[b][v]) for v in range(V + 1)]
            bg = [jnp.broadcast_to(fields[V][i : i + 1, :], (K, COLS)) for i in range(3)]
            start = fields[:V]
            here = start
            history = [start]
            for stage in range(3):
                inc = increments(
                    [pltpu.roll(f, 8, 1) for f in here], here,
                    [pltpu.roll(f, COLS - 8, 1) for f in here],
                    [pltpu.roll(f, 1, 1) for f in here],
                    [pltpu.roll(f, COLS - 1, 1) for f in here], bg,
                )
                here = [advance(stage, start[v], here[v], inc[v]) for v in range(V)]
                history.append(here)
            sides.append(history)
        for stage in range(4):
            for v in range(V):
                left, right = sides[0][stage][v], sides[1][stage][v]
                edges[l, stage, v] = jnp.where(
                    lane8 == 4, pltpu.roll(left, 1, 1), pltpu.roll(right, COLS - 1, 1)
                )

    def stored(l):
        return pltpu.make_async_copy(
            bred.at[l, :, pl.ds(1, ROWS)], bred_hbm.at[l], store_sem.at[l]
        )

    def level(i, pair):
        l = PAIR * pair + i
        for copy in level_copies(l):
            copy.wait_recv()

        def read(stage, v, q):
            if stage == 0:
                return state[l, v, q]
            return (one, two)[stage - 1][v, q]

        for stage in range(3):
            edge = [edges[l, stage, v] for v in range(V)]
            for q in range(1 + stage, 15 - stage):
                bg = [
                    jnp.broadcast_to(bgrows[q // 4, l, pl.ds(v * 4 + q % 4, 1), :], (K, COLS))
                    for v in range(V)
                ]
                here = [read(stage, v, q) for v in range(V)]
                rim = [pltpu.roll(edge[v], (124 - 8 * q) % COLS, 1) for v in range(V)]
                west = [jnp.where(lane == 0, rim[v], pltpu.roll(here[v], 1, 1)) for v in range(V)]
                east = [
                    jnp.where(lane == COLS - 1, rim[v], pltpu.roll(here[v], COLS - 1, 1))
                    for v in range(V)
                ]
                inc = increments(
                    [read(stage, v, q - 1) for v in range(V)], here,
                    [read(stage, v, q + 1) for v in range(V)], west, east, bg,
                )
                for v in range(V):
                    value = advance(stage, state[l, v, q], here[v], inc[v])
                    if stage == 0:
                        one[v, q] = value
                    elif stage == 1:
                        two[v, q] = value
                    else:
                        bred[l, v, q - 3] = value

        sums = [gacc[s] for s in range(SHIFTS)]
        for v in range(V):
            for rr in range(1, 9):
                tile = bred[l, v, rr]
                for s in range(SHIFTS):
                    other = tile if s == 0 else pltpu.roll(tile, K - s, 0)
                    sums[s] = sums[s] + tile * other
        for s in range(SHIFTS):
            gacc[s] = sums[s]

        for v in range(V):
            high, low = split(edges[l, 3, v])
            slots = jnp.where(
                (lane8 == 3) | (lane8 == 4), high,
                jnp.where((lane8 == 5) | (lane8 == 6), pltpu.roll(low, 2, 1), pltpu.roll(high, 4, 1)),
            )
            for rr in range(10):
                moved = pltpu.roll(slots, COLS - 8 * (rr + 3) - 3, 1)
                seams[v, rr] = jnp.where(lane < 6, moved, 0.0)
        high, low = split(bred[l].reshape(M_ROWS, COLS))
        rows = pl.ds(pl.multiple_of(i * M_ROWS, 16), M_ROWS)
        lhs[rows, 0:COLS] = high.astype(jnp.bfloat16)
        lhs[rows, COLS : 2 * COLS] = low.astype(jnp.bfloat16)
        lhs[rows, 2 * COLS : 3 * COLS] = high.astype(jnp.bfloat16)
        lhs[rows, 3 * COLS :] = seams[...].reshape(M_ROWS, COLS).astype(jnp.bfloat16)
        stored(l).start()
        return pair

    def level_pair(pair, carry):
        lax.fori_loop(0, PAIR, level, pair)

        def block(n, carry):
            columns = pl.ds(pl.multiple_of(n * WIDE, WIDE), WIDE)
            mixed = jnp.dot(lhs[...], weights[:, columns], preferred_element_type=jnp.float32)
            for i in range(WIDE // COLS):
                g = n * (WIDE // COLS) + i
                key = keys[g] - pair * (PAIR * 16)
                low = jnp.zeros((K, COLS), jnp.float32)
                high = low
                for at_level in range(PAIR):
                    for v in range(V):
                        before = None
                        for rr in range(10):
                            at = ((at_level * V + v) * 10 + rr) * K
                            value = mixed[at : at + K, i * COLS : (i + 1) * COLS]
                            if before is not None:
                                high = jnp.where(before, value, high)
                            if rr < 9:
                                before = key == v * 64 + at_level * 16 + rr
                                low = jnp.where(before, value, low)
                proj[g] += row_w[g, 0] * low + row_w[g, 1] * high
            return carry

        lax.fori_loop(0, groups * COLS // WIDE, block, 0, unroll=8)
        return carry

    lax.fori_loop(0, L // PAIR, level_pair, 0)
    proj_out = pltpu.make_async_copy(proj, proj_hbm, store_sem.at[L])
    proj_out.start()

    def weigh(g, sums):
        columns = pl.ds(pl.multiple_of(g * COLS, COLS), COLS)
        tile = proj[g]
        scaled = tile / err_ref[0:1, columns]
        return tuple(
            sums[s] + scaled * (tile if s == 0 else pltpu.roll(tile, K - s, 0))
            for s in range(SHIFTS)
        )

    zero = jnp.zeros((K, COLS), jnp.float32)
    normal = lax.fori_loop(0, groups, weigh, (zero,) * SHIFTS, unroll=8)
    mine = zero
    for s in range(SHIFTS):
        total = gacc[s] * (1.0 / cells_all) + normal[s] * (1.0 / obs_all)
        mine = jnp.where(lane == s, jnp.sum(total, axis=1, keepdims=True), mine)

    def all_sum(value, slots, me, peers, device, sends, recvs):
        part[...] = value
        slots[me] = value
        copies = [
            pltpu.make_async_remote_copy(
                src_ref=part, dst_ref=slots.at[me], send_sem=sends.at[d], recv_sem=recvs.at[d],
                device_id=device(peer), device_id_type=MESH,
            )
            for d, peer in enumerate(peers)
        ]
        for copy in copies:
            copy.start()
        for copy in copies:
            copy.wait()
        terms = [slots[i] for i in range(len(peers) + 1)]
        while len(terms) > 1:
            terms = [sum(terms[i : i + 2][1:], terms[i]) for i in range(0, len(terms), 2)]
        return terms[0]

    if direct:
        mine = all_sum(mine, sum_x, gx * n_gy + gy, peers, lambda p: p, xsend, xrecv)
    else:
        mine = all_sum(mine, sum_y, gy, y_peers, lambda p: (gx, p), ysend, yrecv)
        mine = all_sum(mine, sum_x, gx, x_peers, lambda p: (p, gy), xsend, xrecv)

    matrix = jnp.where(lane == sub + K, 1.0, 0.0)
    for s in range(K):
        if s < SHIFTS:
            diagonal = mine[:, s : s + 1]
        else:
            diagonal = pltpu.roll(mine, K - s, 0)[:, K - s : K - s + 1]
        matrix = jnp.where((lane < K) & (((lane - sub) & 7) == s), diagonal, matrix)
    scale = jnp.ones((K, COLS), jnp.float32)
    for j in range(K):
        pivot_row = jnp.broadcast_to(matrix[j : j + 1, :], (K, COLS))
        pivot = jnp.broadcast_to(pivot_row[:, j : j + 1], (K, COLS))
        column = jnp.broadcast_to(matrix[:, j : j + 1], (K, COLS))
        scale = jnp.where(sub == j, pivot, scale)
        matrix = jnp.where(sub > j, matrix - (column / pivot) * pivot_row, matrix)
    matrix = matrix / jnp.sqrt(scale)
    matrix_ref[...] = matrix
    for copy in near:
        copy.wait_send()
    for l in range(L):
        for copy in level_copies(l):
            copy.wait_send()
        stored(l).wait()
    proj_out.wait()


def mix_kernel(
    bred_hbm, proj_hbm, matrix_hbm, err_hbm, out_hbm, obs_hbm,
    bred, proj, matrix_ref, err_ref, out, obs, load_sem, out_sem,
):
    groups = proj.shape[0]
    loads = [
        pltpu.make_async_copy(src, dst, load_sem.at[i])
        for i, (src, dst) in enumerate([(matrix_hbm, matrix_ref), (err_hbm, err_ref), (proj_hbm, proj)])
    ]
    loads += [
        pltpu.make_async_copy(bred_hbm.at[:, v], bred.at[:, v], load_sem.at[3 + v]) for v in range(V)
    ]
    for copy in loads:
        copy.start()
    for copy in loads[:3]:
        copy.wait()
    matrix = matrix_ref[...]
    combo = [jnp.broadcast_to(matrix[:, K + j : K + j + 1], (K, COLS)) for j in range(K)]

    def mix(tile):
        terms = [combo[j] * jnp.broadcast_to(tile[j : j + 1, :], (K, COLS)) for j in range(K)]
        while len(terms) > 1:
            terms = [terms[i] + terms[i + 1] for i in range(0, len(terms), 2)]
        return terms[0]

    def write_obs(g, carry):
        columns = pl.ds(pl.multiple_of(g * COLS, COLS), COLS)
        obs[:, columns] = mix(proj[g]) / jnp.sqrt(err_ref[0:1, columns])
        return carry

    lax.fori_loop(0, groups, write_obs, 0, unroll=8)
    stores = [pltpu.make_async_copy(obs, obs_hbm, out_sem.at[0])]
    stores[0].start()
    part = L * ROWS
    for v in range(V):
        loads[3 + v].wait()
        for l in range(L):
            for r in range(ROWS):
                out[pl.ds(v * K * part + l * ROWS + r, K, stride=part), :] = mix(bred[l, v, r])
        for k in range(K):
            copy = pltpu.make_async_copy(
                out.at[pl.ds((v * K + k) * part, part)],
                out_hbm.at[pl.ds((k * V + v) * part, part)],
                out_sem.at[1 + v * K + k],
            )
            copy.start()
            stores.append(copy)
    for copy in stores:
        copy.wait()


def local(n_gx, n_gy, vectors, background, obs_site, obs_offset, obs_error):
    obs_dev = obs_site.shape[0]
    groups = obs_dev // COLS
    devices = n_gx * n_gy
    body = functools.partial(
        kernel, n_gx, n_gy, float(PLANES * ROWS * COLS * devices), float(obs_dev * devices)
    )
    f32 = jnp.float32
    slots = devices if devices <= 64 else n_gx
    vmem = pl.BlockSpec(memory_space=pltpu.VMEM)
    hbm = pl.BlockSpec(memory_space=pltpu.HBM)
    error = obs_error.reshape(1, obs_dev)
    bred, proj, matrix = pl.pallas_call(
        body,
        out_shape=(
            jax.ShapeDtypeStruct((L, V, ROWS, K, COLS), f32),
            jax.ShapeDtypeStruct((groups, K, COLS), f32),
            jax.ShapeDtypeStruct((K, COLS), f32),
        ),
        in_specs=[hbm] * 5,
        out_specs=(hbm, hbm, vmem),
        scratch_shapes=[
            pltpu.SemaphoreType.DMA((L + 1,)),
            pltpu.VMEM((K * STRIDE, COLS), f32),
            pltpu.VMEM((V * L * ROWS, COLS), f32),
            pltpu.VMEM((groups, COLS), jnp.int32),
            pltpu.VMEM((2, obs_dev), f32),
            pltpu.VMEM((1, obs_dev), f32),
            pltpu.SemaphoreType.DMA((5,)),
            pltpu.VMEM((4 * COLS, obs_dev), jnp.bfloat16),
            pltpu.VMEM((PAIR * M_ROWS, 4 * COLS), jnp.bfloat16),
            pltpu.VMEM((V, 10, K, COLS), f32),
            pltpu.VMEM((groups, K, COLS), jnp.int32),
            pltpu.VMEM((groups, 2, K, COLS), f32),
            pltpu.VMEM((L, V, 16, K, COLS), f32),
            pltpu.VMEM((V, 16, K, COLS), f32),
            pltpu.VMEM((V, 16, K, COLS), f32),
            pltpu.VMEM((L, V, 10, K, COLS), f32),
            pltpu.VMEM((4, L, 16, COLS), f32),
            pltpu.VMEM((3, 4, V + 1, K, COLS), f32),
            pltpu.VMEM((L, 4, V, K, COLS), f32),
            pltpu.VMEM((groups, K, COLS), f32),
            pltpu.VMEM((SHIFTS, K, COLS), f32),
            pltpu.VMEM((n_gy, K, COLS), f32),
            pltpu.VMEM((slots, K, COLS), f32),
            pltpu.VMEM((K, COLS), f32),
            pltpu.SemaphoreType.DMA((N_COPIES,)),
            pltpu.SemaphoreType.DMA((N_COPIES,)),
            pltpu.SemaphoreType.DMA((n_gy - 1,)),
            pltpu.SemaphoreType.DMA((n_gy - 1,)),
            pltpu.SemaphoreType.DMA((slots - 1,)),
            pltpu.SemaphoreType.DMA((slots - 1,)),
        ],
        compiler_params=pltpu.CompilerParams(
            collective_id=0, has_side_effects=True, vmem_limit_bytes=63 * 1024 * 1024
        ),
    )(
        vectors.reshape(K * STRIDE, COLS),
        background.reshape(V * L * ROWS, COLS),
        obs_site.reshape(groups, COLS),
        obs_offset,
        error,
    )
    analysis, obs = pl.pallas_call(
        mix_kernel,
        out_shape=(
            jax.ShapeDtypeStruct((K * STRIDE, COLS), f32),
            jax.ShapeDtypeStruct((K, obs_dev), f32),
        ),
        in_specs=[hbm] * 4,
        out_specs=(hbm, hbm),
        scratch_shapes=[
            pltpu.VMEM((L, V, ROWS, K, COLS), f32),
            pltpu.VMEM((groups, K, COLS), f32),
            pltpu.VMEM((K, COLS), f32),
            pltpu.VMEM((1, obs_dev), f32),
            pltpu.VMEM((K * STRIDE, COLS), f32),
            pltpu.VMEM((K, obs_dev), f32),
            pltpu.SemaphoreType.DMA((3 + V,)),
            pltpu.SemaphoreType.DMA((1 + V * K,)),
        ],
        compiler_params=pltpu.CompilerParams(vmem_limit_bytes=63 * 1024 * 1024),
    )(bred, proj, matrix, error)
    return analysis.reshape(vectors.shape), obs


def solution(mesh):
    placed = (
        P(None, None, None, "gx", "gy"),
        P(None, None, "gx", "gy"),
        P(("gx", "gy")),
        P(None, ("gx", "gy")),
        P(("gx", "gy")),
    )
    return jax.shard_map(
        functools.partial(local, mesh.shape["gx"], mesh.shape["gy"]),
        mesh=mesh,
        in_specs=placed,
        out_specs=(P(None, None, None, "gx", "gy"), P(None, ("gx", "gy"))),
        check_vma=False,
    )
```

```python
import functools

import jax
import jax.numpy as jnp
from jax import lax
from jax.experimental import pallas as pl
from jax.experimental.pallas import tpu as pltpu
from jax.sharding import PartitionSpec as P

K = 8
V = 3
L = 4
ROWS = 8
COLS = 128
PLANES = V * L
STRIDE = PLANES * ROWS
STEP = 0.35
MESH = pl.DeviceIdType.MESH
SHIFTS = 5
N_EDGE = 8
M_ROWS = V * 10 * K
WIDE = 256
PAIR = 2
N_COPIES = N_EDGE + 2 + 2 * L


def increments(below, here, above, west, east, bg):
    wx, wy, va = bg
    dx = [above[i] - below[i] for i in range(V)]
    dy = [east[i] - west[i] for i in range(V)]
    half = 0.5 * STEP
    hx, hy, sv = half * wx, half * wy, STEP * va
    inc_e = sv * here[1] - (hx * dx[0] + hy * dy[0]) - half * dx[2]
    inc_n = -(sv * here[0]) - (hx * dx[1] + hy * dy[1]) - half * dy[2]
    inc_h = -(hx * dx[2] + hy * dy[2]) - half * (dx[0] + dy[1])
    return inc_e, inc_n, inc_h


def advance(stage, start, here, inc):
    if stage == 0:
        return here + inc
    if stage == 1:
        return 0.75 * start + 0.25 * (here + inc)
    return (1.0 / 3.0) * start + (2.0 / 3.0) * (here + inc)


def split(value):
    high = value.astype(jnp.bfloat16).astype(jnp.float32)
    return high, value - high


def kernel(
    n_gx, n_gy, cells_all, obs_all,
    vec_hbm, bg_hbm, site_hbm, off_hbm, err_hbm,
    bred_hbm, proj_hbm, matrix_ref, store_sem,
    vec_ref, bg_ref, site_ref, off_ref, err_ref, load_sem,
    weights, lhs, seams, keys, row_w,
    state, one, two, bred, bgrows, strips, edges, proj, gacc, sum_y, sum_x, part,
    send_sem, recv_sem, ysend, yrecv, xsend, xrecv,
):
    groups = proj.shape[0]
    gx = lax.axis_index("gx")
    gy = lax.axis_index("gy")
    up, dn = lax.rem(gx + n_gx - 1, n_gx), lax.rem(gx + 1, n_gx)
    lf, rt = lax.rem(gy + n_gy - 1, n_gy), lax.rem(gy + 1, n_gy)
    x_peers = [lax.rem(gx + d, n_gx) for d in range(1, n_gx)]
    y_peers = [lax.rem(gy + d, n_gy) for d in range(1, n_gy)]
    lane = lax.broadcasted_iota(jnp.int32, (K, COLS), 1)
    sub = lax.broadcasted_iota(jnp.int32, (K, COLS), 0)
    lane8 = lane & 7

    loads = [
        pltpu.make_async_copy(src, dst, load_sem.at[i])
        for i, (src, dst) in enumerate(
            [(bg_hbm, bg_ref), (vec_hbm, vec_ref), (site_hbm, site_ref),
             (off_hbm, off_ref), (err_hbm, err_ref)]
        )
    ]
    for copy in loads:
        copy.start()

    barrier = pltpu.get_barrier_semaphore()
    greeted = [(a, b) for a in (up, dn) for b in (lf, rt)]
    direct = sum_x.shape[0] == n_gx * n_gy
    if direct:
        peers = [
            (lax.rem(gx + i, n_gx), lax.rem(gy + j, n_gy))
            for i in range(n_gx) for j in range(n_gy) if i + j > 0
        ]
        greeted = peers
    else:
        greeted += [(a, gy) for a in x_peers] + [(gx, b) for b in y_peers]
    for peer in greeted:
        pl.semaphore_signal(barrier, inc=1, device_id=peer, device_id_type=MESH)

    loads[0].wait()
    loads[1].wait()
    packed = [[jnp.zeros((K, COLS), jnp.float32) for _ in range(V + 1)] for _ in range(2)]
    for l in range(L):
        for r in range(ROWS):
            h, base = r // 4, l * 32 + (r % 4) * 8
            put = (lane >> 3) == base // 8
            for v in range(V):
                tile = vec_ref[pl.ds((v * L + l) * ROWS + r, K, stride=STRIDE), :]
                state[l, v, 4 + r] = tile
                packed[h][v] = jnp.where(put, pltpu.roll(tile, (base + 4) % COLS, 1), packed[h][v])
            rows = [
                jnp.broadcast_to(bg_ref[pl.ds((v * L + l) * ROWS + r, 1), :], (K, COLS))
                for v in range(V)
            ]
            tile = jnp.where(sub == 0, rows[0], jnp.where(sub == 1, rows[1], rows[2]))
            packed[h][V] = jnp.where(put, pltpu.roll(tile, (base + 4) % COLS, 1), packed[h][V])
        for h in range(2):
            for v in range(V):
                bgrows[1 + h, l, pl.ds(v * 4, 4), :] = bg_ref[pl.ds((v * L + l) * ROWS + h * 4, 4), :]
            bgrows[1 + h, l, pl.ds(12, 4), :] = jnp.zeros((4, COLS), jnp.float32)
    for h in range(2):
        for v in range(V + 1):
            strips[1, 1 + h, v] = packed[h][v]

    pl.semaphore_wait(barrier, len(greeted))

    def remote(src, dst, index, peer):
        return pltpu.make_async_remote_copy(
            src_ref=src, dst_ref=dst, send_sem=send_sem.at[index], recv_sem=recv_sem.at[index],
            device_id=peer, device_id_type=MESH,
        )

    both = pl.ds(1, 2)
    near = [
        remote(strips.at[1, 1], strips.at[1, 3], 0, (up, gy)),
        remote(strips.at[1, 2], strips.at[1, 0], 1, (dn, gy)),
        remote(strips.at[1, 1], strips.at[2, 3], 2, (up, lf)),
        remote(strips.at[1, 1], strips.at[0, 3], 3, (up, rt)),
        remote(strips.at[1, 2], strips.at[2, 0], 4, (dn, lf)),
        remote(strips.at[1, 2], strips.at[0, 0], 5, (dn, rt)),
        remote(strips.at[1, both], strips.at[2, both], 6, (gx, lf)),
        remote(strips.at[1, both], strips.at[0, both], 7, (gx, rt)),
        remote(bgrows.at[1], bgrows.at[3], 8, (up, gy)),
        remote(bgrows.at[2], bgrows.at[0], 9, (dn, gy)),
    ]

    def level_copies(l):
        return (
            remote(state.at[l, :, pl.ds(4, 4)], state.at[l, :, pl.ds(12, 4)], 10 + 2 * l, (up, gy)),
            remote(state.at[l, :, pl.ds(8, 4)], state.at[l, :, pl.ds(0, 4)], 11 + 2 * l, (dn, gy)),
        )

    for copy in near:
        copy.start()
    for l in range(PAIR):
        for copy in level_copies(l):
            copy.start()

    gacc[...] = jnp.zeros_like(gacc)
    proj[...] = jnp.zeros_like(proj)
    for copy in loads[2:]:
        copy.wait()

    cell = lax.broadcasted_iota(jnp.int32, (COLS, COLS), 0)
    slot = lax.broadcasted_iota(jnp.int32, (16, COLS), 0)
    weights[pl.ds(3 * COLS, COLS), :] = jnp.zeros((COLS, groups * COLS), jnp.bfloat16)

    def weigh_columns(g, carry):
        columns = pl.ds(pl.multiple_of(g * COLS, COLS), COLS)
        site = site_ref[pl.ds(g, 1), :]
        a, b = off_ref[0:1, columns], off_ref[1:2, columns]
        row, col = (site >> 7) & 7, site & 127
        abs_a, abs_b = jnp.abs(a), jnp.abs(b)
        row0 = jnp.where(a < 0.0, row - 1, row)
        col0 = jnp.where(b < 0.0, col - 1, col)
        keys[g] = jnp.broadcast_to((site >> 10) * 16 + row0 + 1, (K, COLS))
        row_w[g, 0] = jnp.broadcast_to(jnp.where(a < 0.0, abs_a, 1.0 - abs_a), (K, COLS))
        row_w[g, 1] = jnp.broadcast_to(jnp.where(a < 0.0, 1.0 - abs_a, abs_a), (K, COLS))
        w0 = jnp.where(b < 0.0, abs_b, 1.0 - abs_b)
        w1 = jnp.where(b < 0.0, 1.0 - abs_b, abs_b)
        high, low = split(
            jnp.where(cell == col0, w0, 0.0) + jnp.where(cell == col0 + 1, w1, 0.0)
        )
        weights[pl.ds(0, COLS), columns] = high.astype(jnp.bfloat16)
        weights[pl.ds(COLS, COLS), columns] = high.astype(jnp.bfloat16)
        weights[pl.ds(2 * COLS, COLS), columns] = low.astype(jnp.bfloat16)
        at_left = jnp.where(col0 < 0, w0, 0.0)
        at_right = jnp.where(col0 >= COLS - 1, w1, 0.0)
        high, low = split(jnp.where((slot & 1) == 0, at_right, at_left))
        seam = jnp.where(slot < 4, high, jnp.where(slot < 6, low, 0.0))
        weights[pl.ds(3 * COLS, 16), columns] = seam.astype(jnp.bfloat16)
        return carry

    lax.fori_loop(0, groups, weigh_columns, 0)
    for l in range(PAIR):
        for copy in level_copies(l):
            copy.wait_send()
    for l in range(PAIR, L):
        for copy in level_copies(l):
            copy.start()
    for copy in near:
        copy.wait_recv()

    for l in range(L):
        whole = []
        for side in range(3):
            fields = []
            for v in range(V + 1):
                tile = jnp.zeros((K, COLS), jnp.float32)
                for seg in range(4):
                    moved = pltpu.roll(strips[side, seg, v], (seg + 4 - l) * 32 % COLS, 1)
                    tile = jnp.where((lane >> 5) == seg, moved, tile)
                fields.append(tile)
            whole.append(fields)
        inner = lane8 < 4
        sides = []
        for a, b in ((0, 1), (1, 2)):
            fields = [jnp.where(inner, whole[a][v], whole[b][v]) for v in range(V + 1)]
            bg = [jnp.broadcast_to(fields[V][i : i + 1, :], (K, COLS)) for i in range(3)]
            start = fields[:V]
            here = start
            history = [start]
            for stage in range(3):
                inc = increments(
                    [pltpu.roll(f, 8, 1) for f in here], here,
                    [pltpu.roll(f, COLS - 8, 1) for f in here],
                    [pltpu.roll(f, 1, 1) for f in here],
                    [pltpu.roll(f, COLS - 1, 1) for f in here], bg,
                )
                here = [advance(stage, start[v], here[v], inc[v]) for v in range(V)]
                history.append(here)
            sides.append(history)
        for stage in range(4):
            for v in range(V):
                left, right = sides[0][stage][v], sides[1][stage][v]
                edges[l, stage, v] = jnp.where(
                    lane8 == 4, pltpu.roll(left, 1, 1), pltpu.roll(right, COLS - 1, 1)
                )

    def stored(l):
        return pltpu.make_async_copy(
            bred.at[l, :, pl.ds(1, ROWS)], bred_hbm.at[l], store_sem.at[l]
        )

    def level(i, pair):
        l = PAIR * pair + i
        for copy in level_copies(l):
            copy.wait_recv()

        def read(stage, v, q):
            if stage == 0:
                return state[l, v, q]
            return (one, two)[stage - 1][v, q]

        for stage in range(3):
            edge = [edges[l, stage, v] for v in range(V)]
            for q in range(1 + stage, 15 - stage):
                bg = [
                    jnp.broadcast_to(bgrows[q // 4, l, pl.ds(v * 4 + q % 4, 1), :], (K, COLS))
                    for v in range(V)
                ]
                here = [read(stage, v, q) for v in range(V)]
                rim = [pltpu.roll(edge[v], (124 - 8 * q) % COLS, 1) for v in range(V)]
                west = [jnp.where(lane == 0, rim[v], pltpu.roll(here[v], 1, 1)) for v in range(V)]
                east = [
                    jnp.where(lane == COLS - 1, rim[v], pltpu.roll(here[v], COLS - 1, 1))
                    for v in range(V)
                ]
                inc = increments(
                    [read(stage, v, q - 1) for v in range(V)], here,
                    [read(stage, v, q + 1) for v in range(V)], west, east, bg,
                )
                for v in range(V):
                    value = advance(stage, state[l, v, q], here[v], inc[v])
                    if stage == 0:
                        one[v, q] = value
                    elif stage == 1:
                        two[v, q] = value
                    else:
                        bred[l, v, q - 3] = value

        sums = [gacc[s] for s in range(SHIFTS)]
        for v in range(V):
            for rr in range(1, 9):
                tile = bred[l, v, rr]
                for s in range(SHIFTS):
                    other = tile if s == 0 else pltpu.roll(tile, K - s, 0)
                    sums[s] = sums[s] + tile * other
        for s in range(SHIFTS):
            gacc[s] = sums[s]

        for v in range(V):
            high, low = split(edges[l, 3, v])
            slots = jnp.where(
                (lane8 == 3) | (lane8 == 4), high,
                jnp.where((lane8 == 5) | (lane8 == 6), pltpu.roll(low, 2, 1), pltpu.roll(high, 4, 1)),
            )
            for rr in range(10):
                moved = pltpu.roll(slots, COLS - 8 * (rr + 3) - 3, 1)
                seams[v, rr] = jnp.where(lane < 6, moved, 0.0)
        high, low = split(bred[l].reshape(M_ROWS, COLS))
        rows = pl.ds(pl.multiple_of(i * M_ROWS, 16), M_ROWS)
        lhs[rows, 0:COLS] = high.astype(jnp.bfloat16)
        lhs[rows, COLS : 2 * COLS] = low.astype(jnp.bfloat16)
        lhs[rows, 2 * COLS : 3 * COLS] = high.astype(jnp.bfloat16)
        lhs[rows, 3 * COLS :] = seams[...].reshape(M_ROWS, COLS).astype(jnp.bfloat16)
        stored(l).start()
        return pair

    def level_pair(pair, carry):
        lax.fori_loop(0, PAIR, level, pair)

        def block(n, carry):
            columns = pl.ds(pl.multiple_of(n * WIDE, WIDE), WIDE)
            mixed = jnp.dot(lhs[...], weights[:, columns], preferred_element_type=jnp.float32)
            for i in range(WIDE // COLS):
                g = n * (WIDE // COLS) + i
                key = keys[g] - pair * (PAIR * 16)
                low = jnp.zeros((K, COLS), jnp.float32)
                high = low
                for at_level in range(PAIR):
                    for v in range(V):
                        before = None
                        for rr in range(10):
                            at = ((at_level * V + v) * 10 + rr) * K
                            value = mixed[at : at + K, i * COLS : (i + 1) * COLS]
                            if before is not None:
                                high = jnp.where(before, value, high)
                            if rr < 9:
                                before = key == v * 64 + at_level * 16 + rr
                                low = jnp.where(before, value, low)
                proj[g] += row_w[g, 0] * low + row_w[g, 1] * high
            return carry

        lax.fori_loop(0, groups * COLS // WIDE, block, 0, unroll=8)
        return carry

    lax.fori_loop(0, L // PAIR, level_pair, 0)
    proj_out = pltpu.make_async_copy(proj, proj_hbm, store_sem.at[L])
    proj_out.start()

    def weigh(g, sums):
        columns = pl.ds(pl.multiple_of(g * COLS, COLS), COLS)
        tile = proj[g]
        scaled = tile / err_ref[0:1, columns]
        return tuple(
            sums[s] + scaled * (tile if s == 0 else pltpu.roll(tile, K - s, 0))
            for s in range(SHIFTS)
        )

    zero = jnp.zeros((K, COLS), jnp.float32)
    normal = lax.fori_loop(0, groups, weigh, (zero,) * SHIFTS, unroll=8)
    mine = zero
    for s in range(SHIFTS):
        total = gacc[s] * (1.0 / cells_all) + normal[s] * (1.0 / obs_all)
        mine = jnp.where(lane == s, jnp.sum(total, axis=1, keepdims=True), mine)

    def all_sum(value, slots, me, peers, device, sends, recvs):
        part[...] = value
        slots[me] = value
        copies = [
            pltpu.make_async_remote_copy(
                src_ref=part, dst_ref=slots.at[me], send_sem=sends.at[d], recv_sem=recvs.at[d],
                device_id=device(peer), device_id_type=MESH,
            )
            for d, peer in enumerate(peers)
        ]
        for copy in copies:
            copy.start()
        for copy in copies:
            copy.wait()
        terms = [slots[i] for i in range(len(peers) + 1)]
        while len(terms) > 1:
            terms = [sum(terms[i : i + 2][1:], terms[i]) for i in range(0, len(terms), 2)]
        return terms[0]

    if direct:
        mine = all_sum(mine, sum_x, gx * n_gy + gy, peers, lambda p: p, xsend, xrecv)
    else:
        mine = all_sum(mine, sum_y, gy, y_peers, lambda p: (gx, p), ysend, yrecv)
        mine = all_sum(mine, sum_x, gx, x_peers, lambda p: (p, gy), xsend, xrecv)

    matrix = jnp.where(lane == sub + K, 1.0, 0.0)
    for s in range(K):
        if s < SHIFTS:
            diagonal = mine[:, s : s + 1]
        else:
            diagonal = pltpu.roll(mine, K - s, 0)[:, K - s : K - s + 1]
        matrix = jnp.where((lane < K) & (((lane - sub) & 7) == s), diagonal, matrix)
    scale = jnp.ones((K, COLS), jnp.float32)
    for j in range(K):
        pivot_row = jnp.broadcast_to(matrix[j : j + 1, :], (K, COLS))
        pivot = jnp.broadcast_to(pivot_row[:, j : j + 1], (K, COLS))
        column = jnp.broadcast_to(matrix[:, j : j + 1], (K, COLS))
        scale = jnp.where(sub == j, pivot, scale)
        matrix = jnp.where(sub > j, matrix - (column / pivot) * pivot_row, matrix)
    matrix = matrix / jnp.sqrt(scale)
    matrix_ref[...] = matrix
    for copy in near:
        copy.wait_send()
    for l in range(L):
        if l >= PAIR:
            for copy in level_copies(l):
                copy.wait_send()
        stored(l).wait()
    proj_out.wait()


def mix_kernel(
    bred_hbm, proj_hbm, matrix_hbm, err_hbm, out_hbm, obs_hbm,
    bred, proj, matrix_ref, err_ref, out, obs, load_sem, out_sem,
):
    groups = proj.shape[0]
    loads = [
        pltpu.make_async_copy(src, dst, load_sem.at[i])
        for i, (src, dst) in enumerate([(matrix_hbm, matrix_ref), (err_hbm, err_ref), (proj_hbm, proj)])
    ]
    loads += [
        pltpu.make_async_copy(bred_hbm.at[:, v], bred.at[:, v], load_sem.at[3 + v]) for v in range(V)
    ]
    for copy in loads:
        copy.start()
    for copy in loads[:3]:
        copy.wait()
    matrix = matrix_ref[...]
    combo = [jnp.broadcast_to(matrix[:, K + j : K + j + 1], (K, COLS)) for j in range(K)]

    def mix(tile):
        terms = [combo[j] * jnp.broadcast_to(tile[j : j + 1, :], (K, COLS)) for j in range(K)]
        while len(terms) > 1:
            terms = [terms[i] + terms[i + 1] for i in range(0, len(terms), 2)]
        return terms[0]

    def write_obs(g, carry):
        columns = pl.ds(pl.multiple_of(g * COLS, COLS), COLS)
        obs[:, columns] = mix(proj[g]) / jnp.sqrt(err_ref[0:1, columns])
        return carry

    lax.fori_loop(0, groups, write_obs, 0, unroll=8)
    stores = [pltpu.make_async_copy(obs, obs_hbm, out_sem.at[0])]
    stores[0].start()
    part = L * ROWS
    for v in range(V):
        loads[3 + v].wait()
        for l in range(L):
            for r in range(ROWS):
                out[pl.ds(v * K * part + l * ROWS + r, K, stride=part), :] = mix(bred[l, v, r])
        for k in range(K):
            copy = pltpu.make_async_copy(
                out.at[pl.ds((v * K + k) * part, part)],
                out_hbm.at[pl.ds((k * V + v) * part, part)],
                out_sem.at[1 + v * K + k],
            )
            copy.start()
            stores.append(copy)
    for copy in stores:
        copy.wait()


def local(n_gx, n_gy, vectors, background, obs_site, obs_offset, obs_error):
    obs_dev = obs_site.shape[0]
    groups = obs_dev // COLS
    devices = n_gx * n_gy
    body = functools.partial(
        kernel, n_gx, n_gy, float(PLANES * ROWS * COLS * devices), float(obs_dev * devices)
    )
    f32 = jnp.float32
    slots = devices if devices <= 64 else n_gx
    vmem = pl.BlockSpec(memory_space=pltpu.VMEM)
    hbm = pl.BlockSpec(memory_space=pltpu.HBM)
    error = obs_error.reshape(1, obs_dev)
    bred, proj, matrix = pl.pallas_call(
        body,
        out_shape=(
            jax.ShapeDtypeStruct((L, V, ROWS, K, COLS), f32),
            jax.ShapeDtypeStruct((groups, K, COLS), f32),
            jax.ShapeDtypeStruct((K, COLS), f32),
        ),
        in_specs=[hbm] * 5,
        out_specs=(hbm, hbm, vmem),
        scratch_shapes=[
            pltpu.SemaphoreType.DMA((L + 1,)),
            pltpu.VMEM((K * STRIDE, COLS), f32),
            pltpu.VMEM((V * L * ROWS, COLS), f32),
            pltpu.VMEM((groups, COLS), jnp.int32),
            pltpu.VMEM((2, obs_dev), f32),
            pltpu.VMEM((1, obs_dev), f32),
            pltpu.SemaphoreType.DMA((5,)),
            pltpu.VMEM((4 * COLS, obs_dev), jnp.bfloat16),
            pltpu.VMEM((PAIR * M_ROWS, 4 * COLS), jnp.bfloat16),
            pltpu.VMEM((V, 10, K, COLS), f32),
            pltpu.VMEM((groups, K, COLS), jnp.int32),
            pltpu.VMEM((groups, 2, K, COLS), f32),
            pltpu.VMEM((L, V, 16, K, COLS), f32),
            pltpu.VMEM((V, 16, K, COLS), f32),
            pltpu.VMEM((V, 16, K, COLS), f32),
            pltpu.VMEM((L, V, 10, K, COLS), f32),
            pltpu.VMEM((4, L, 16, COLS), f32),
            pltpu.VMEM((3, 4, V + 1, K, COLS), f32),
            pltpu.VMEM((L, 4, V, K, COLS), f32),
            pltpu.VMEM((groups, K, COLS), f32),
            pltpu.VMEM((SHIFTS, K, COLS), f32),
            pltpu.VMEM((n_gy, K, COLS), f32),
            pltpu.VMEM((slots, K, COLS), f32),
            pltpu.VMEM((K, COLS), f32),
            pltpu.SemaphoreType.DMA((N_COPIES,)),
            pltpu.SemaphoreType.DMA((N_COPIES,)),
            pltpu.SemaphoreType.DMA((n_gy - 1,)),
            pltpu.SemaphoreType.DMA((n_gy - 1,)),
            pltpu.SemaphoreType.DMA((slots - 1,)),
            pltpu.SemaphoreType.DMA((slots - 1,)),
        ],
        compiler_params=pltpu.CompilerParams(
            collective_id=0, has_side_effects=True, vmem_limit_bytes=63 * 1024 * 1024
        ),
    )(
        vectors.reshape(K * STRIDE, COLS),
        background.reshape(V * L * ROWS, COLS),
        obs_site.reshape(groups, COLS),
        obs_offset,
        error,
    )
    analysis, obs = pl.pallas_call(
        mix_kernel,
        out_shape=(
            jax.ShapeDtypeStruct((K * STRIDE, COLS), f32),
            jax.ShapeDtypeStruct((K, obs_dev), f32),
        ),
        in_specs=[hbm] * 4,
        out_specs=(hbm, hbm),
        scratch_shapes=[
            pltpu.VMEM((L, V, ROWS, K, COLS), f32),
            pltpu.VMEM((groups, K, COLS), f32),
            pltpu.VMEM((K, COLS), f32),
            pltpu.VMEM((1, obs_dev), f32),
            pltpu.VMEM((K * STRIDE, COLS), f32),
            pltpu.VMEM((K, obs_dev), f32),
            pltpu.SemaphoreType.DMA((3 + V,)),
            pltpu.SemaphoreType.DMA((1 + V * K,)),
        ],
        compiler_params=pltpu.CompilerParams(vmem_limit_bytes=63 * 1024 * 1024),
    )(bred, proj, matrix, error)
    return analysis.reshape(vectors.shape), obs


def solution(mesh):
    placed = (
        P(None, None, None, "gx", "gy"),
        P(None, None, "gx", "gy"),
        P(("gx", "gy")),
        P(None, ("gx", "gy")),
        P(("gx", "gy")),
    )
    return jax.shard_map(
        functools.partial(local, mesh.shape["gx"], mesh.shape["gy"]),
        mesh=mesh,
        in_specs=placed,
        out_specs=(P(None, None, None, "gx", "gy"), P(None, ("gx", "gy"))),
        check_vma=False,
    )
```

```python
import functools

import jax
import jax.numpy as jnp
from jax import lax
from jax.experimental import pallas as pl
from jax.experimental.pallas import tpu as pltpu
from jax.sharding import PartitionSpec as P

K = 8
V = 3
L = 4
ROWS = 8
COLS = 128
PLANES = V * L
STRIDE = PLANES * ROWS
STEP = 0.35
MESH = pl.DeviceIdType.MESH
SHIFTS = 5
N_EDGE = 8
M_ROWS = V * 10 * K
WIDE = 256
PAIR = 2
N_COPIES = N_EDGE + 2 + 2 * L


def increments(below, here, above, west, east, bg):
    wx, wy, va = bg
    dx = [above[i] - below[i] for i in range(V)]
    dy = [east[i] - west[i] for i in range(V)]
    half = 0.5 * STEP
    hx, hy, sv = half * wx, half * wy, STEP * va
    inc_e = sv * here[1] - (hx * dx[0] + hy * dy[0]) - half * dx[2]
    inc_n = -(sv * here[0]) - (hx * dx[1] + hy * dy[1]) - half * dy[2]
    inc_h = -(hx * dx[2] + hy * dy[2]) - half * (dx[0] + dy[1])
    return inc_e, inc_n, inc_h


def advance(stage, start, here, inc):
    if stage == 0:
        return here + inc
    if stage == 1:
        return 0.75 * start + 0.25 * (here + inc)
    return (1.0 / 3.0) * start + (2.0 / 3.0) * (here + inc)


def split(value):
    high = value.astype(jnp.bfloat16).astype(jnp.float32)
    return high, value - high


def kernel(
    n_gx, n_gy, cells_all, obs_all,
    vec_hbm, bg_hbm, site_hbm, off_hbm, err_hbm,
    bred_hbm, proj_hbm, matrix_ref, store_sem,
    vec_ref, bg_ref, site_ref, off_ref, err_ref, load_sem,
    weights, lhs, seams, keys, row_w,
    state, one, two, bred, bgrows, strips, edges, proj, gacc, sum_y, sum_x, part,
    send_sem, recv_sem, ysend, yrecv, xsend, xrecv,
):
    groups = proj.shape[0]
    gx = lax.axis_index("gx")
    gy = lax.axis_index("gy")
    up, dn = lax.rem(gx + n_gx - 1, n_gx), lax.rem(gx + 1, n_gx)
    lf, rt = lax.rem(gy + n_gy - 1, n_gy), lax.rem(gy + 1, n_gy)
    x_peers = [lax.rem(gx + d, n_gx) for d in range(1, n_gx)]
    y_peers = [lax.rem(gy + d, n_gy) for d in range(1, n_gy)]
    lane = lax.broadcasted_iota(jnp.int32, (K, COLS), 1)
    sub = lax.broadcasted_iota(jnp.int32, (K, COLS), 0)
    lane8 = lane & 7

    loads = [
        pltpu.make_async_copy(src, dst, load_sem.at[i])
        for i, (src, dst) in enumerate(
            [(bg_hbm, bg_ref), (vec_hbm, vec_ref), (site_hbm, site_ref),
             (off_hbm, off_ref), (err_hbm, err_ref)]
        )
    ]
    for copy in loads:
        copy.start()

    barrier = pltpu.get_barrier_semaphore()
    greeted = [(a, b) for a in (up, dn) for b in (lf, rt)]
    direct = sum_x.shape[0] == n_gx * n_gy
    if direct:
        peers = [
            (lax.rem(gx + i, n_gx), lax.rem(gy + j, n_gy))
            for i in range(n_gx) for j in range(n_gy) if i + j > 0
        ]
        greeted = peers
    else:
        greeted += [(a, gy) for a in x_peers] + [(gx, b) for b in y_peers]
    for peer in greeted:
        pl.semaphore_signal(barrier, inc=1, device_id=peer, device_id_type=MESH)

    loads[0].wait()
    loads[1].wait()
    packed = [[jnp.zeros((K, COLS), jnp.float32) for _ in range(V + 1)] for _ in range(2)]
    for l in range(L):
        for r in range(ROWS):
            h, base = r // 4, l * 32 + (r % 4) * 8
            put = (lane >> 3) == base // 8
            for v in range(V):
                tile = vec_ref[pl.ds((v * L + l) * ROWS + r, K, stride=STRIDE), :]
                state[l, v, 4 + r] = tile
                packed[h][v] = jnp.where(put, pltpu.roll(tile, (base + 4) % COLS, 1), packed[h][v])
            rows = [
                jnp.broadcast_to(bg_ref[pl.ds((v * L + l) * ROWS + r, 1), :], (K, COLS))
                for v in range(V)
            ]
            tile = jnp.where(sub == 0, rows[0], jnp.where(sub == 1, rows[1], rows[2]))
            packed[h][V] = jnp.where(put, pltpu.roll(tile, (base + 4) % COLS, 1), packed[h][V])
        for h in range(2):
            for v in range(V):
                bgrows[1 + h, l, pl.ds(v * 4, 4), :] = bg_ref[pl.ds((v * L + l) * ROWS + h * 4, 4), :]
            bgrows[1 + h, l, pl.ds(12, 4), :] = jnp.zeros((4, COLS), jnp.float32)
    for h in range(2):
        for v in range(V + 1):
            strips[1, 1 + h, v] = packed[h][v]

    pl.semaphore_wait(barrier, len(greeted))

    def remote(src, dst, index, peer):
        return pltpu.make_async_remote_copy(
            src_ref=src, dst_ref=dst, send_sem=send_sem.at[index], recv_sem=recv_sem.at[index],
            device_id=peer, device_id_type=MESH,
        )

    both = pl.ds(1, 2)
    near = [
        remote(strips.at[1, 1], strips.at[1, 3], 0, (up, gy)),
        remote(strips.at[1, 2], strips.at[1, 0], 1, (dn, gy)),
        remote(strips.at[1, 1], strips.at[2, 3], 2, (up, lf)),
        remote(strips.at[1, 1], strips.at[0, 3], 3, (up, rt)),
        remote(strips.at[1, 2], strips.at[2, 0], 4, (dn, lf)),
        remote(strips.at[1, 2], strips.at[0, 0], 5, (dn, rt)),
        remote(strips.at[1, both], strips.at[2, both], 6, (gx, lf)),
        remote(strips.at[1, both], strips.at[0, both], 7, (gx, rt)),
        remote(bgrows.at[1], bgrows.at[3], 8, (up, gy)),
        remote(bgrows.at[2], bgrows.at[0], 9, (dn, gy)),
    ]

    def level_copies(l):
        return (
            remote(state.at[l, :, pl.ds(4, 4)], state.at[l, :, pl.ds(12, 4)], 10 + 2 * l, (up, gy)),
            remote(state.at[l, :, pl.ds(8, 4)], state.at[l, :, pl.ds(0, 4)], 11 + 2 * l, (dn, gy)),
        )

    for copy in near:
        copy.start()
    for l in range(PAIR):
        for copy in level_copies(l):
            copy.start()

    gacc[...] = jnp.zeros_like(gacc)
    proj[...] = jnp.zeros_like(proj)
    for copy in loads[2:]:
        copy.wait()

    cell = lax.broadcasted_iota(jnp.int32, (COLS, COLS), 0)
    slot = lax.broadcasted_iota(jnp.int32, (16, COLS), 0)
    weights[pl.ds(3 * COLS, COLS), :] = jnp.zeros((COLS, groups * COLS), jnp.bfloat16)

    def weigh_columns(g, carry):
        columns = pl.ds(pl.multiple_of(g * COLS, COLS), COLS)
        site = site_ref[pl.ds(g, 1), :]
        a, b = off_ref[0:1, columns], off_ref[1:2, columns]
        row, col = (site >> 7) & 7, site & 127
        abs_a, abs_b = jnp.abs(a), jnp.abs(b)
        row0 = jnp.where(a < 0.0, row - 1, row)
        col0 = jnp.where(b < 0.0, col - 1, col)
        keys[g] = jnp.broadcast_to((site >> 10) * 16 + row0 + 1, (K, COLS))
        row_w[g, 0] = jnp.broadcast_to(jnp.where(a < 0.0, abs_a, 1.0 - abs_a), (K, COLS))
        row_w[g, 1] = jnp.broadcast_to(jnp.where(a < 0.0, 1.0 - abs_a, abs_a), (K, COLS))
        w0 = jnp.where(b < 0.0, abs_b, 1.0 - abs_b)
        w1 = jnp.where(b < 0.0, 1.0 - abs_b, abs_b)
        high, low = split(
            jnp.where(cell == col0, w0, 0.0) + jnp.where(cell == col0 + 1, w1, 0.0)
        )
        weights[pl.ds(0, COLS), columns] = high.astype(jnp.bfloat16)
        weights[pl.ds(COLS, COLS), columns] = high.astype(jnp.bfloat16)
        weights[pl.ds(2 * COLS, COLS), columns] = low.astype(jnp.bfloat16)
        at_left = jnp.where(col0 < 0, w0, 0.0)
        at_right = jnp.where(col0 >= COLS - 1, w1, 0.0)
        high, low = split(jnp.where((slot & 1) == 0, at_right, at_left))
        seam = jnp.where(slot < 4, high, jnp.where(slot < 6, low, 0.0))
        weights[pl.ds(3 * COLS, 16), columns] = seam.astype(jnp.bfloat16)
        return carry

    lax.fori_loop(0, groups, weigh_columns, 0)
    for l in range(PAIR):
        for copy in level_copies(l):
            copy.wait_send()
    for l in range(PAIR, L):
        for copy in level_copies(l):
            copy.start()
    for copy in near:
        copy.wait_recv()

    for l in range(L):
        whole = []
        for side in range(3):
            fields = []
            for v in range(V + 1):
                tile = jnp.zeros((K, COLS), jnp.float32)
                for seg in range(4):
                    moved = pltpu.roll(strips[side, seg, v], (seg + 4 - l) * 32 % COLS, 1)
                    tile = jnp.where((lane >> 5) == seg, moved, tile)
                fields.append(tile)
            whole.append(fields)
        inner = lane8 < 4
        sides = []
        for a, b in ((0, 1), (1, 2)):
            fields = [jnp.where(inner, whole[a][v], whole[b][v]) for v in range(V + 1)]
            bg = [jnp.broadcast_to(fields[V][i : i + 1, :], (K, COLS)) for i in range(3)]
            start = fields[:V]
            here = start
            history = [start]
            for stage in range(3):
                inc = increments(
                    [pltpu.roll(f, 8, 1) for f in here], here,
                    [pltpu.roll(f, COLS - 8, 1) for f in here],
                    [pltpu.roll(f, 1, 1) for f in here],
                    [pltpu.roll(f, COLS - 1, 1) for f in here], bg,
                )
                here = [advance(stage, start[v], here[v], inc[v]) for v in range(V)]
                history.append(here)
            sides.append(history)
        for stage in range(4):
            for v in range(V):
                left, right = sides[0][stage][v], sides[1][stage][v]
                edges[l, stage, v] = jnp.where(
                    lane8 == 4, pltpu.roll(left, 1, 1), pltpu.roll(right, COLS - 1, 1)
                )

    def stored(l):
        return pltpu.make_async_copy(
            bred.at[l, :, pl.ds(1, ROWS)], bred_hbm.at[l], store_sem.at[l]
        )

    def level(i, pair):
        l = PAIR * pair + i

        def read(stage, v, q):
            if stage == 0:
                return state[l, v, q]
            return (one, two)[stage - 1][i, v, q]

        for stage in range(3):
            edge = [edges[l, stage, v] for v in range(V)]
            for q in range(1 + stage, 15 - stage):
                bg = [
                    jnp.broadcast_to(bgrows[q // 4, l, pl.ds(v * 4 + q % 4, 1), :], (K, COLS))
                    for v in range(V)
                ]
                here = [read(stage, v, q) for v in range(V)]
                rim = [pltpu.roll(edge[v], (124 - 8 * q) % COLS, 1) for v in range(V)]
                west = [jnp.where(lane == 0, rim[v], pltpu.roll(here[v], 1, 1)) for v in range(V)]
                east = [
                    jnp.where(lane == COLS - 1, rim[v], pltpu.roll(here[v], COLS - 1, 1))
                    for v in range(V)
                ]
                inc = increments(
                    [read(stage, v, q - 1) for v in range(V)], here,
                    [read(stage, v, q + 1) for v in range(V)], west, east, bg,
                )
                for v in range(V):
                    value = advance(stage, state[l, v, q], here[v], inc[v])
                    if stage == 0:
                        one[i, v, q] = value
                    elif stage == 1:
                        two[i, v, q] = value
                    else:
                        bred[l, v, q - 3] = value

        sums = [gacc[s] for s in range(SHIFTS)]
        for v in range(V):
            for rr in range(1, 9):
                tile = bred[l, v, rr]
                for s in range(SHIFTS):
                    other = tile if s == 0 else pltpu.roll(tile, K - s, 0)
                    sums[s] = sums[s] + tile * other
        for s in range(SHIFTS):
            gacc[s] = sums[s]

        for v in range(V):
            high, low = split(edges[l, 3, v])
            slots = jnp.where(
                (lane8 == 3) | (lane8 == 4), high,
                jnp.where((lane8 == 5) | (lane8 == 6), pltpu.roll(low, 2, 1), pltpu.roll(high, 4, 1)),
            )
            for rr in range(10):
                moved = pltpu.roll(slots, COLS - 8 * (rr + 3) - 3, 1)
                seams[i, v, rr] = jnp.where(lane < 6, moved, 0.0)
        high, low = split(bred[l].reshape(M_ROWS, COLS))
        rows = pl.ds(i * M_ROWS, M_ROWS)
        lhs[rows, 0:COLS] = high.astype(jnp.bfloat16)
        lhs[rows, COLS : 2 * COLS] = low.astype(jnp.bfloat16)
        lhs[rows, 2 * COLS : 3 * COLS] = high.astype(jnp.bfloat16)
        lhs[rows, 3 * COLS :] = seams[i].reshape(M_ROWS, COLS).astype(jnp.bfloat16)
        stored(l).start()

    def level_pair(pair, carry):
        for i in range(PAIR):
            for copy in level_copies(PAIR * pair + i):
                copy.wait_recv()
        for i in range(PAIR):
            level(i, pair)

        def block(n, carry):
            columns = pl.ds(pl.multiple_of(n * WIDE, WIDE), WIDE)
            mixed = jnp.dot(lhs[...], weights[:, columns], preferred_element_type=jnp.float32)
            for i in range(WIDE // COLS):
                g = n * (WIDE // COLS) + i
                key = keys[g] - pair * (PAIR * 16)
                low = jnp.zeros((K, COLS), jnp.float32)
                high = low
                for at_level in range(PAIR):
                    for v in range(V):
                        before = None
                        for rr in range(10):
                            at = ((at_level * V + v) * 10 + rr) * K
                            value = mixed[at : at + K, i * COLS : (i + 1) * COLS]
                            if before is not None:
                                high = jnp.where(before, value, high)
                            if rr < 9:
                                before = key == v * 64 + at_level * 16 + rr
                                low = jnp.where(before, value, low)
                proj[g] += row_w[g, 0] * low + row_w[g, 1] * high
            return carry

        lax.fori_loop(0, groups * COLS // WIDE, block, 0, unroll=16)
        return carry

    lax.fori_loop(0, L // PAIR, level_pair, 0)
    proj_out = pltpu.make_async_copy(proj, proj_hbm, store_sem.at[L])
    proj_out.start()

    def weigh(g, sums):
        columns = pl.ds(pl.multiple_of(g * COLS, COLS), COLS)
        tile = proj[g]
        scaled = tile / err_ref[0:1, columns]
        return tuple(
            sums[s] + scaled * (tile if s == 0 else pltpu.roll(tile, K - s, 0))
            for s in range(SHIFTS)
        )

    zero = jnp.zeros((K, COLS), jnp.float32)
    normal = lax.fori_loop(0, groups, weigh, (zero,) * SHIFTS, unroll=8)
    mine = zero
    for s in range(SHIFTS):
        total = gacc[s] * (1.0 / cells_all) + normal[s] * (1.0 / obs_all)
        mine = jnp.where(lane == s, jnp.sum(total, axis=1, keepdims=True), mine)

    def all_sum(value, slots, me, peers, device, sends, recvs):
        part[...] = value
        slots[me] = value
        copies = [
            pltpu.make_async_remote_copy(
                src_ref=part, dst_ref=slots.at[me], send_sem=sends.at[d], recv_sem=recvs.at[d],
                device_id=device(peer), device_id_type=MESH,
            )
            for d, peer in enumerate(peers)
        ]
        for copy in copies:
            copy.start()
        for copy in copies:
            copy.wait()
        terms = [slots[i] for i in range(len(peers) + 1)]
        while len(terms) > 1:
            terms = [sum(terms[i : i + 2][1:], terms[i]) for i in range(0, len(terms), 2)]
        return terms[0]

    if direct:
        mine = all_sum(mine, sum_x, gx * n_gy + gy, peers, lambda p: p, xsend, xrecv)
    else:
        mine = all_sum(mine, sum_y, gy, y_peers, lambda p: (gx, p), ysend, yrecv)
        mine = all_sum(mine, sum_x, gx, x_peers, lambda p: (p, gy), xsend, xrecv)

    matrix = jnp.where(lane == sub + K, 1.0, 0.0)
    for s in range(K):
        if s < SHIFTS:
            diagonal = mine[:, s : s + 1]
        else:
            diagonal = pltpu.roll(mine, K - s, 0)[:, K - s : K - s + 1]
        matrix = jnp.where((lane < K) & (((lane - sub) & 7) == s), diagonal, matrix)
    scale = jnp.ones((K, COLS), jnp.float32)
    for j in range(K):
        pivot_row = jnp.broadcast_to(matrix[j : j + 1, :], (K, COLS))
        pivot = jnp.broadcast_to(pivot_row[:, j : j + 1], (K, COLS))
        column = jnp.broadcast_to(matrix[:, j : j + 1], (K, COLS))
        scale = jnp.where(sub == j, pivot, scale)
        matrix = jnp.where(sub > j, matrix - (column / pivot) * pivot_row, matrix)
    matrix = matrix / jnp.sqrt(scale)
    matrix_ref[...] = matrix
    for copy in near:
        copy.wait_send()
    for l in range(L):
        if l >= PAIR:
            for copy in level_copies(l):
                copy.wait_send()
        stored(l).wait()
    proj_out.wait()


def mix_kernel(
    bred_hbm, proj_hbm, matrix_hbm, err_hbm, out_hbm, obs_hbm,
    bred, proj, matrix_ref, err_ref, out, obs, load_sem, out_sem,
):
    groups = proj.shape[0]
    loads = [
        pltpu.make_async_copy(src, dst, load_sem.at[i])
        for i, (src, dst) in enumerate([(matrix_hbm, matrix_ref), (err_hbm, err_ref), (proj_hbm, proj)])
    ]
    loads += [
        pltpu.make_async_copy(bred_hbm.at[:, v], bred.at[:, v], load_sem.at[3 + v]) for v in range(V)
    ]
    for copy in loads:
        copy.start()
    for copy in loads[:3]:
        copy.wait()
    matrix = matrix_ref[...]
    combo = [jnp.broadcast_to(matrix[:, K + j : K + j + 1], (K, COLS)) for j in range(K)]

    def mix(tile):
        terms = [combo[j] * jnp.broadcast_to(tile[j : j + 1, :], (K, COLS)) for j in range(K)]
        while len(terms) > 1:
            terms = [terms[i] + terms[i + 1] for i in range(0, len(terms), 2)]
        return terms[0]

    def write_obs(g, carry):
        columns = pl.ds(pl.multiple_of(g * COLS, COLS), COLS)
        obs[:, columns] = mix(proj[g]) / jnp.sqrt(err_ref[0:1, columns])
        return carry

    lax.fori_loop(0, groups, write_obs, 0, unroll=8)
    stores = [pltpu.make_async_copy(obs, obs_hbm, out_sem.at[0])]
    stores[0].start()
    part = L * ROWS
    for v in range(V):
        loads[3 + v].wait()
        for l in range(L):
            for r in range(ROWS):
                out[pl.ds(v * K * part + l * ROWS + r, K, stride=part), :] = mix(bred[l, v, r])
        for k in range(K):
            copy = pltpu.make_async_copy(
                out.at[pl.ds((v * K + k) * part, part)],
                out_hbm.at[pl.ds((k * V + v) * part, part)],
                out_sem.at[1 + v * K + k],
            )
            copy.start()
            stores.append(copy)
    for copy in stores:
        copy.wait()


def local(n_gx, n_gy, vectors, background, obs_site, obs_offset, obs_error):
    obs_dev = obs_site.shape[0]
    groups = obs_dev // COLS
    devices = n_gx * n_gy
    body = functools.partial(
        kernel, n_gx, n_gy, float(PLANES * ROWS * COLS * devices), float(obs_dev * devices)
    )
    f32 = jnp.float32
    slots = devices if devices <= 64 else n_gx
    vmem = pl.BlockSpec(memory_space=pltpu.VMEM)
    hbm = pl.BlockSpec(memory_space=pltpu.HBM)
    error = obs_error.reshape(1, obs_dev)
    bred, proj, matrix = pl.pallas_call(
        body,
        out_shape=(
            jax.ShapeDtypeStruct((L, V, ROWS, K, COLS), f32),
            jax.ShapeDtypeStruct((groups, K, COLS), f32),
            jax.ShapeDtypeStruct((K, COLS), f32),
        ),
        in_specs=[hbm] * 5,
        out_specs=(hbm, hbm, vmem),
        scratch_shapes=[
            pltpu.SemaphoreType.DMA((L + 1,)),
            pltpu.VMEM((K * STRIDE, COLS), f32),
            pltpu.VMEM((V * L * ROWS, COLS), f32),
            pltpu.VMEM((groups, COLS), jnp.int32),
            pltpu.VMEM((2, obs_dev), f32),
            pltpu.VMEM((1, obs_dev), f32),
            pltpu.SemaphoreType.DMA((5,)),
            pltpu.VMEM((4 * COLS, obs_dev), jnp.bfloat16),
            pltpu.VMEM((PAIR * M_ROWS, 4 * COLS), jnp.bfloat16),
            pltpu.VMEM((PAIR, V, 10, K, COLS), f32),
            pltpu.VMEM((groups, K, COLS), jnp.int32),
            pltpu.VMEM((groups, 2, K, COLS), f32),
            pltpu.VMEM((L, V, 16, K, COLS), f32),
            pltpu.VMEM((PAIR, V, 16, K, COLS), f32),
            pltpu.VMEM((PAIR, V, 16, K, COLS), f32),
            pltpu.VMEM((L, V, 10, K, COLS), f32),
            pltpu.VMEM((4, L, 16, COLS), f32),
            pltpu.VMEM((3, 4, V + 1, K, COLS), f32),
            pltpu.VMEM((L, 4, V, K, COLS), f32),
            pltpu.VMEM((groups, K, COLS), f32),
            pltpu.VMEM((SHIFTS, K, COLS), f32),
            pltpu.VMEM((n_gy, K, COLS), f32),
            pltpu.VMEM((slots, K, COLS), f32),
            pltpu.VMEM((K, COLS), f32),
            pltpu.SemaphoreType.DMA((N_COPIES,)),
            pltpu.SemaphoreType.DMA((N_COPIES,)),
            pltpu.SemaphoreType.DMA((n_gy - 1,)),
            pltpu.SemaphoreType.DMA((n_gy - 1,)),
            pltpu.SemaphoreType.DMA((slots - 1,)),
            pltpu.SemaphoreType.DMA((slots - 1,)),
        ],
        compiler_params=pltpu.CompilerParams(
            collective_id=0, has_side_effects=True, vmem_limit_bytes=63 * 1024 * 1024
        ),
    )(
        vectors.reshape(K * STRIDE, COLS),
        background.reshape(V * L * ROWS, COLS),
        obs_site.reshape(groups, COLS),
        obs_offset,
        error,
    )
    analysis, obs = pl.pallas_call(
        mix_kernel,
        out_shape=(
            jax.ShapeDtypeStruct((K * STRIDE, COLS), f32),
            jax.ShapeDtypeStruct((K, obs_dev), f32),
        ),
        in_specs=[hbm] * 4,
        out_specs=(hbm, hbm),
        scratch_shapes=[
            pltpu.VMEM((L, V, ROWS, K, COLS), f32),
            pltpu.VMEM((groups, K, COLS), f32),
            pltpu.VMEM((K, COLS), f32),
            pltpu.VMEM((1, obs_dev), f32),
            pltpu.VMEM((K * STRIDE, COLS), f32),
            pltpu.VMEM((K, obs_dev), f32),
            pltpu.SemaphoreType.DMA((3 + V,)),
            pltpu.SemaphoreType.DMA((1 + V * K,)),
        ],
        compiler_params=pltpu.CompilerParams(vmem_limit_bytes=63 * 1024 * 1024),
    )(bred, proj, matrix, error)
    return analysis.reshape(vectors.shape), obs


def solution(mesh):
    placed = (
        P(None, None, None, "gx", "gy"),
        P(None, None, "gx", "gy"),
        P(("gx", "gy")),
        P(None, ("gx", "gy")),
        P(("gx", "gy")),
    )
    return jax.shard_map(
        functools.partial(local, mesh.shape["gx"], mesh.shape["gy"]),
        mesh=mesh,
        in_specs=placed,
        out_specs=(P(None, None, None, "gx", "gy"), P(None, ("gx", "gy"))),
        check_vma=False,
    )
```

```python
import functools

import jax
import jax.numpy as jnp
from jax import lax
from jax.experimental import pallas as pl
from jax.experimental.pallas import tpu as pltpu
from jax.sharding import PartitionSpec as P

K = 8
V = 3
L = 4
ROWS = 8
COLS = 128
PLANES = V * L
STRIDE = PLANES * ROWS
STEP = 0.35
MESH = pl.DeviceIdType.MESH
SHIFTS = 5
N_EDGE = 8
M_ROWS = V * 10 * K
WIDE = 256
PAIR = 2
N_COPIES = N_EDGE + 2 + 2 * L


def increments(below, here, above, west, east, bg):
    wx, wy, va = bg
    dx = [above[i] - below[i] for i in range(V)]
    dy = [east[i] - west[i] for i in range(V)]
    half = 0.5 * STEP
    hx, hy, sv = half * wx, half * wy, STEP * va
    inc_e = sv * here[1] - (hx * dx[0] + hy * dy[0]) - half * dx[2]
    inc_n = -(sv * here[0]) - (hx * dx[1] + hy * dy[1]) - half * dy[2]
    inc_h = -(hx * dx[2] + hy * dy[2]) - half * (dx[0] + dy[1])
    return inc_e, inc_n, inc_h


def advance(stage, start, here, inc):
    if stage == 0:
        return here + inc
    if stage == 1:
        return 0.75 * start + 0.25 * (here + inc)
    return (1.0 / 3.0) * start + (2.0 / 3.0) * (here + inc)


def split(value):
    high = value.astype(jnp.bfloat16).astype(jnp.float32)
    return high, value - high


def kernel(
    n_gx, n_gy, cells_all, obs_all,
    vec_hbm, bg_hbm, site_hbm, off_hbm, err_hbm,
    bred_hbm, proj_hbm, matrix_ref, store_sem,
    vec_ref, bg_ref, site_ref, off_ref, err_ref, load_sem,
    weights, lhs, seams, keys, row_w,
    state, one, two, bred, bgrows, strips, edges, proj, gacc, sum_y, sum_x, part,
    send_sem, recv_sem, ysend, yrecv, xsend, xrecv,
):
    groups = proj.shape[0]
    gx = lax.axis_index("gx")
    gy = lax.axis_index("gy")
    up, dn = lax.rem(gx + n_gx - 1, n_gx), lax.rem(gx + 1, n_gx)
    lf, rt = lax.rem(gy + n_gy - 1, n_gy), lax.rem(gy + 1, n_gy)
    x_peers = [lax.rem(gx + d, n_gx) for d in range(1, n_gx)]
    y_peers = [lax.rem(gy + d, n_gy) for d in range(1, n_gy)]
    lane = lax.broadcasted_iota(jnp.int32, (K, COLS), 1)
    sub = lax.broadcasted_iota(jnp.int32, (K, COLS), 0)
    lane8 = lane & 7

    loads = [
        pltpu.make_async_copy(src, dst, load_sem.at[i])
        for i, (src, dst) in enumerate(
            [(bg_hbm, bg_ref), (vec_hbm, vec_ref), (site_hbm, site_ref),
             (off_hbm, off_ref), (err_hbm, err_ref)]
        )
    ]
    for copy in loads:
        copy.start()

    barrier = pltpu.get_barrier_semaphore()
    greeted = [(a, b) for a in (up, dn) for b in (lf, rt)]
    direct = sum_x.shape[0] == n_gx * n_gy
    if direct:
        peers = [
            (lax.rem(gx + i, n_gx), lax.rem(gy + j, n_gy))
            for i in range(n_gx) for j in range(n_gy) if i + j > 0
        ]
        greeted = peers
    else:
        greeted += [(a, gy) for a in x_peers] + [(gx, b) for b in y_peers]
    for peer in greeted:
        pl.semaphore_signal(barrier, inc=1, device_id=peer, device_id_type=MESH)

    loads[0].wait()
    loads[1].wait()
    packed = [[jnp.zeros((K, COLS), jnp.float32) for _ in range(V + 1)] for _ in range(2)]
    for l in range(L):
        for r in range(ROWS):
            h, base = r // 4, l * 32 + (r % 4) * 8
            put = (lane >> 3) == base // 8
            for v in range(V):
                tile = vec_ref[pl.ds((v * L + l) * ROWS + r, K, stride=STRIDE), :]
                state[l, v, 4 + r] = tile
                packed[h][v] = jnp.where(put, pltpu.roll(tile, (base + 4) % COLS, 1), packed[h][v])
            rows = [
                jnp.broadcast_to(bg_ref[pl.ds((v * L + l) * ROWS + r, 1), :], (K, COLS))
                for v in range(V)
            ]
            tile = jnp.where(sub == 0, rows[0], jnp.where(sub == 1, rows[1], rows[2]))
            packed[h][V] = jnp.where(put, pltpu.roll(tile, (base + 4) % COLS, 1), packed[h][V])
        for h in range(2):
            for v in range(V):
                bgrows[1 + h, l, pl.ds(v * 4, 4), :] = bg_ref[pl.ds((v * L + l) * ROWS + h * 4, 4), :]
            bgrows[1 + h, l, pl.ds(12, 4), :] = jnp.zeros((4, COLS), jnp.float32)
    for h in range(2):
        for v in range(V + 1):
            strips[1, 1 + h, v] = packed[h][v]

    pl.semaphore_wait(barrier, len(greeted))

    def remote(src, dst, index, peer):
        return pltpu.make_async_remote_copy(
            src_ref=src, dst_ref=dst, send_sem=send_sem.at[index], recv_sem=recv_sem.at[index],
            device_id=peer, device_id_type=MESH,
        )

    both = pl.ds(1, 2)
    near = [
        remote(strips.at[1, 1], strips.at[1, 3], 0, (up, gy)),
        remote(strips.at[1, 2], strips.at[1, 0], 1, (dn, gy)),
        remote(strips.at[1, 1], strips.at[2, 3], 2, (up, lf)),
        remote(strips.at[1, 1], strips.at[0, 3], 3, (up, rt)),
        remote(strips.at[1, 2], strips.at[2, 0], 4, (dn, lf)),
        remote(strips.at[1, 2], strips.at[0, 0], 5, (dn, rt)),
        remote(strips.at[1, both], strips.at[2, both], 6, (gx, lf)),
        remote(strips.at[1, both], strips.at[0, both], 7, (gx, rt)),
        remote(bgrows.at[1], bgrows.at[3], 8, (up, gy)),
        remote(bgrows.at[2], bgrows.at[0], 9, (dn, gy)),
    ]

    def level_copies(l):
        return (
            remote(state.at[l, :, pl.ds(4, 4)], state.at[l, :, pl.ds(12, 4)], 10 + 2 * l, (up, gy)),
            remote(state.at[l, :, pl.ds(8, 4)], state.at[l, :, pl.ds(0, 4)], 11 + 2 * l, (dn, gy)),
        )

    for copy in near:
        copy.start()
    for l in range(PAIR):
        for copy in level_copies(l):
            copy.start()

    gacc[...] = jnp.zeros_like(gacc)
    proj[...] = jnp.zeros_like(proj)
    for copy in loads[2:]:
        copy.wait()

    cell = lax.broadcasted_iota(jnp.int32, (COLS, COLS), 0)
    slot = lax.broadcasted_iota(jnp.int32, (16, COLS), 0)
    weights[pl.ds(3 * COLS, COLS), :] = jnp.zeros((COLS, groups * COLS), jnp.bfloat16)

    def weigh_columns(g, carry):
        columns = pl.ds(pl.multiple_of(g * COLS, COLS), COLS)
        site = site_ref[pl.ds(g, 1), :]
        a, b = off_ref[0:1, columns], off_ref[1:2, columns]
        row, col = (site >> 7) & 7, site & 127
        abs_a, abs_b = jnp.abs(a), jnp.abs(b)
        row0 = jnp.where(a < 0.0, row - 1, row)
        col0 = jnp.where(b < 0.0, col - 1, col)
        keys[g] = jnp.broadcast_to((site >> 10) * 16 + row0 + 1, (K, COLS))
        row_w[g, 0] = jnp.broadcast_to(jnp.where(a < 0.0, abs_a, 1.0 - abs_a), (K, COLS))
        row_w[g, 1] = jnp.broadcast_to(jnp.where(a < 0.0, 1.0 - abs_a, abs_a), (K, COLS))
        w0 = jnp.where(b < 0.0, abs_b, 1.0 - abs_b)
        w1 = jnp.where(b < 0.0, 1.0 - abs_b, abs_b)
        high, low = split(
            jnp.where(cell == col0, w0, 0.0) + jnp.where(cell == col0 + 1, w1, 0.0)
        )
        weights[pl.ds(0, COLS), columns] = high.astype(jnp.bfloat16)
        weights[pl.ds(COLS, COLS), columns] = high.astype(jnp.bfloat16)
        weights[pl.ds(2 * COLS, COLS), columns] = low.astype(jnp.bfloat16)
        at_left = jnp.where(col0 < 0, w0, 0.0)
        at_right = jnp.where(col0 >= COLS - 1, w1, 0.0)
        high, low = split(jnp.where((slot & 1) == 0, at_right, at_left))
        seam = jnp.where(slot < 4, high, jnp.where(slot < 6, low, 0.0))
        weights[pl.ds(3 * COLS, 16), columns] = seam.astype(jnp.bfloat16)
        return carry

    lax.fori_loop(0, groups, weigh_columns, 0)
    for copy in near:
        copy.wait_recv()

    for l in range(L):
        whole = []
        for side in range(3):
            fields = []
            for v in range(V + 1):
                tile = jnp.zeros((K, COLS), jnp.float32)
                for seg in range(4):
                    moved = pltpu.roll(strips[side, seg, v], (seg + 4 - l) * 32 % COLS, 1)
                    tile = jnp.where((lane >> 5) == seg, moved, tile)
                fields.append(tile)
            whole.append(fields)
        inner = lane8 < 4
        sides = []
        for a, b in ((0, 1), (1, 2)):
            fields = [jnp.where(inner, whole[a][v], whole[b][v]) for v in range(V + 1)]
            bg = [jnp.broadcast_to(fields[V][i : i + 1, :], (K, COLS)) for i in range(3)]
            start = fields[:V]
            here = start
            history = [start]
            for stage in range(3):
                inc = increments(
                    [pltpu.roll(f, 8, 1) for f in here], here,
                    [pltpu.roll(f, COLS - 8, 1) for f in here],
                    [pltpu.roll(f, 1, 1) for f in here],
                    [pltpu.roll(f, COLS - 1, 1) for f in here], bg,
                )
                here = [advance(stage, start[v], here[v], inc[v]) for v in range(V)]
                history.append(here)
            sides.append(history)
        for stage in range(4):
            for v in range(V):
                left, right = sides[0][stage][v], sides[1][stage][v]
                edges[l, stage, v] = jnp.where(
                    lane8 == 4, pltpu.roll(left, 1, 1), pltpu.roll(right, COLS - 1, 1)
                )

    for l in range(PAIR):
        for copy in level_copies(l):
            copy.wait_send()
    for l in range(PAIR, L):
        for copy in level_copies(l):
            copy.start()

    def stored(l):
        return pltpu.make_async_copy(
            bred.at[l, :, pl.ds(1, ROWS)], bred_hbm.at[l], store_sem.at[l]
        )

    def level(i, pair):
        l = PAIR * pair + i
        for copy in level_copies(l):
            copy.wait_recv()

        def read(stage, v, q):
            if stage == 0:
                return state[l, v, q]
            return (one, two)[stage - 1][v, q]

        for stage in range(3):
            edge = [edges[l, stage, v] for v in range(V)]
            for q in range(1 + stage, 15 - stage):
                bg = [
                    jnp.broadcast_to(bgrows[q // 4, l, pl.ds(v * 4 + q % 4, 1), :], (K, COLS))
                    for v in range(V)
                ]
                here = [read(stage, v, q) for v in range(V)]
                rim = [pltpu.roll(edge[v], (124 - 8 * q) % COLS, 1) for v in range(V)]
                west = [jnp.where(lane == 0, rim[v], pltpu.roll(here[v], 1, 1)) for v in range(V)]
                east = [
                    jnp.where(lane == COLS - 1, rim[v], pltpu.roll(here[v], COLS - 1, 1))
                    for v in range(V)
                ]
                inc = increments(
                    [read(stage, v, q - 1) for v in range(V)], here,
                    [read(stage, v, q + 1) for v in range(V)], west, east, bg,
                )
                for v in range(V):
                    value = advance(stage, state[l, v, q], here[v], inc[v])
                    if stage == 0:
                        one[v, q] = value
                    elif stage == 1:
                        two[v, q] = value
                    else:
                        bred[l, v, q - 3] = value

        sums = [gacc[s] for s in range(SHIFTS)]
        for v in range(V):
            for rr in range(1, 9):
                tile = bred[l, v, rr]
                for s in range(SHIFTS):
                    other = tile if s == 0 else pltpu.roll(tile, K - s, 0)
                    sums[s] = sums[s] + tile * other
        for s in range(SHIFTS):
            gacc[s] = sums[s]

        for v in range(V):
            high, low = split(edges[l, 3, v])
            slots = jnp.where(
                (lane8 == 3) | (lane8 == 4), high,
                jnp.where((lane8 == 5) | (lane8 == 6), pltpu.roll(low, 2, 1), pltpu.roll(high, 4, 1)),
            )
            for rr in range(10):
                moved = pltpu.roll(slots, COLS - 8 * (rr + 3) - 3, 1)
                seams[v, rr] = jnp.where(lane < 6, moved, 0.0)
        high, low = split(bred[l].reshape(M_ROWS, COLS))
        rows = pl.ds(pl.multiple_of(i * M_ROWS, 16), M_ROWS)
        lhs[rows, 0:COLS] = high.astype(jnp.bfloat16)
        lhs[rows, COLS : 2 * COLS] = low.astype(jnp.bfloat16)
        lhs[rows, 2 * COLS : 3 * COLS] = high.astype(jnp.bfloat16)
        lhs[rows, 3 * COLS :] = seams[...].reshape(M_ROWS, COLS).astype(jnp.bfloat16)
        stored(l).start()
        return pair

    def level_pair(pair, carry):
        lax.fori_loop(0, PAIR, level, pair)

        def block(n, carry):
            columns = pl.ds(pl.multiple_of(n * WIDE, WIDE), WIDE)
            mixed = jnp.dot(lhs[...], weights[:, columns], preferred_element_type=jnp.float32)
            for i in range(WIDE // COLS):
                g = n * (WIDE // COLS) + i
                key = keys[g] - pair * (PAIR * 16)
                low = jnp.zeros((K, COLS), jnp.float32)
                high = low
                for at_level in range(PAIR):
                    for v in range(V):
                        before = None
                        for rr in range(10):
                            at = ((at_level * V + v) * 10 + rr) * K
                            value = mixed[at : at + K, i * COLS : (i + 1) * COLS]
                            if before is not None:
                                high = jnp.where(before, value, high)
                            if rr < 9:
                                before = key == v * 64 + at_level * 16 + rr
                                low = jnp.where(before, value, low)
                proj[g] += row_w[g, 0] * low + row_w[g, 1] * high
            return carry

        lax.fori_loop(0, groups * COLS // WIDE, block, 0, unroll=8)
        return carry

    lax.fori_loop(0, L // PAIR, level_pair, 0)
    proj_out = pltpu.make_async_copy(proj, proj_hbm, store_sem.at[L])
    proj_out.start()

    def weigh(g, sums):
        columns = pl.ds(pl.multiple_of(g * COLS, COLS), COLS)
        tile = proj[g]
        scaled = tile / err_ref[0:1, columns]
        return tuple(
            sums[s] + scaled * (tile if s == 0 else pltpu.roll(tile, K - s, 0))
            for s in range(SHIFTS)
        )

    zero = jnp.zeros((K, COLS), jnp.float32)
    normal = lax.fori_loop(0, groups, weigh, (zero,) * SHIFTS, unroll=8)
    mine = zero
    for s in range(SHIFTS):
        total = gacc[s] * (1.0 / cells_all) + normal[s] * (1.0 / obs_all)
        mine = jnp.where(lane == s, jnp.sum(total, axis=1, keepdims=True), mine)

    def all_sum(value, slots, me, peers, device, sends, recvs):
        part[...] = value
        slots[me] = value
        copies = [
            pltpu.make_async_remote_copy(
                src_ref=part, dst_ref=slots.at[me], send_sem=sends.at[d], recv_sem=recvs.at[d],
                device_id=device(peer), device_id_type=MESH,
            )
            for d, peer in enumerate(peers)
        ]
        for copy in copies:
            copy.start()
        for copy in copies:
            copy.wait()
        terms = [slots[i] for i in range(len(peers) + 1)]
        while len(terms) > 1:
            terms = [sum(terms[i : i + 2][1:], terms[i]) for i in range(0, len(terms), 2)]
        return terms[0]

    if direct:
        mine = all_sum(mine, sum_x, gx * n_gy + gy, peers, lambda p: p, xsend, xrecv)
    else:
        mine = all_sum(mine, sum_y, gy, y_peers, lambda p: (gx, p), ysend, yrecv)
        mine = all_sum(mine, sum_x, gx, x_peers, lambda p: (p, gy), xsend, xrecv)

    matrix = jnp.where(lane == sub + K, 1.0, 0.0)
    for s in range(K):
        if s < SHIFTS:
            diagonal = mine[:, s : s + 1]
        else:
            diagonal = pltpu.roll(mine, K - s, 0)[:, K - s : K - s + 1]
        matrix = jnp.where((lane < K) & (((lane - sub) & 7) == s), diagonal, matrix)
    scale = jnp.ones((K, COLS), jnp.float32)
    for j in range(K):
        pivot_row = jnp.broadcast_to(matrix[j : j + 1, :], (K, COLS))
        pivot = jnp.broadcast_to(pivot_row[:, j : j + 1], (K, COLS))
        column = jnp.broadcast_to(matrix[:, j : j + 1], (K, COLS))
        scale = jnp.where(sub == j, pivot, scale)
        matrix = jnp.where(sub > j, matrix - (column / pivot) * pivot_row, matrix)
    matrix = matrix / jnp.sqrt(scale)
    matrix_ref[...] = matrix
    for copy in near:
        copy.wait_send()
    for l in range(L):
        if l >= PAIR:
            for copy in level_copies(l):
                copy.wait_send()
        stored(l).wait()
    proj_out.wait()


def mix_kernel(
    bred_hbm, proj_hbm, matrix_hbm, err_hbm, out_hbm, obs_hbm,
    bred, proj, matrix_ref, err_ref, out, obs, load_sem, out_sem,
):
    groups = proj.shape[0]
    loads = [
        pltpu.make_async_copy(src, dst, load_sem.at[i])
        for i, (src, dst) in enumerate([(matrix_hbm, matrix_ref), (err_hbm, err_ref), (proj_hbm, proj)])
    ]
    loads += [
        pltpu.make_async_copy(bred_hbm.at[:, v], bred.at[:, v], load_sem.at[3 + v]) for v in range(V)
    ]
    for copy in loads:
        copy.start()
    for copy in loads[:3]:
        copy.wait()
    matrix = matrix_ref[...]
    combo = [jnp.broadcast_to(matrix[:, K + j : K + j + 1], (K, COLS)) for j in range(K)]

    def mix(tile):
        terms = [combo[j] * jnp.broadcast_to(tile[j : j + 1, :], (K, COLS)) for j in range(K)]
        while len(terms) > 1:
            terms = [terms[i] + terms[i + 1] for i in range(0, len(terms), 2)]
        return terms[0]

    def write_obs(g, carry):
        columns = pl.ds(pl.multiple_of(g * COLS, COLS), COLS)
        obs[:, columns] = mix(proj[g]) / jnp.sqrt(err_ref[0:1, columns])
        return carry

    lax.fori_loop(0, groups, write_obs, 0, unroll=8)
    stores = [pltpu.make_async_copy(obs, obs_hbm, out_sem.at[0])]
    stores[0].start()
    part = L * ROWS
    for v in range(V):
        loads[3 + v].wait()
        for l in range(L):
            for r in range(ROWS):
                out[pl.ds(v * K * part + l * ROWS + r, K, stride=part), :] = mix(bred[l, v, r])
        for k in range(K):
            copy = pltpu.make_async_copy(
                out.at[pl.ds((v * K + k) * part, part)],
                out_hbm.at[pl.ds((k * V + v) * part, part)],
                out_sem.at[1 + v * K + k],
            )
            copy.start()
            stores.append(copy)
    for copy in stores:
        copy.wait()


def local(n_gx, n_gy, vectors, background, obs_site, obs_offset, obs_error):
    obs_dev = obs_site.shape[0]
    groups = obs_dev // COLS
    devices = n_gx * n_gy
    body = functools.partial(
        kernel, n_gx, n_gy, float(PLANES * ROWS * COLS * devices), float(obs_dev * devices)
    )
    f32 = jnp.float32
    slots = devices if devices <= 64 else n_gx
    vmem = pl.BlockSpec(memory_space=pltpu.VMEM)
    hbm = pl.BlockSpec(memory_space=pltpu.HBM)
    error = obs_error.reshape(1, obs_dev)
    bred, proj, matrix = pl.pallas_call(
        body,
        out_shape=(
            jax.ShapeDtypeStruct((L, V, ROWS, K, COLS), f32),
            jax.ShapeDtypeStruct((groups, K, COLS), f32),
            jax.ShapeDtypeStruct((K, COLS), f32),
        ),
        in_specs=[hbm] * 5,
        out_specs=(hbm, hbm, vmem),
        scratch_shapes=[
            pltpu.SemaphoreType.DMA((L + 1,)),
            pltpu.VMEM((K * STRIDE, COLS), f32),
            pltpu.VMEM((V * L * ROWS, COLS), f32),
            pltpu.VMEM((groups, COLS), jnp.int32),
            pltpu.VMEM((2, obs_dev), f32),
            pltpu.VMEM((1, obs_dev), f32),
            pltpu.SemaphoreType.DMA((5,)),
            pltpu.VMEM((4 * COLS, obs_dev), jnp.bfloat16),
            pltpu.VMEM((PAIR * M_ROWS, 4 * COLS), jnp.bfloat16),
            pltpu.VMEM((V, 10, K, COLS), f32),
            pltpu.VMEM((groups, K, COLS), jnp.int32),
            pltpu.VMEM((groups, 2, K, COLS), f32),
            pltpu.VMEM((L, V, 16, K, COLS), f32),
            pltpu.VMEM((V, 16, K, COLS), f32),
            pltpu.VMEM((V, 16, K, COLS), f32),
            pltpu.VMEM((L, V, 10, K, COLS), f32),
            pltpu.VMEM((4, L, 16, COLS), f32),
            pltpu.VMEM((3, 4, V + 1, K, COLS), f32),
            pltpu.VMEM((L, 4, V, K, COLS), f32),
            pltpu.VMEM((groups, K, COLS), f32),
            pltpu.VMEM((SHIFTS, K, COLS), f32),
            pltpu.VMEM((n_gy, K, COLS), f32),
            pltpu.VMEM((slots, K, COLS), f32),
            pltpu.VMEM((K, COLS), f32),
            pltpu.SemaphoreType.DMA((N_COPIES,)),
            pltpu.SemaphoreType.DMA((N_COPIES,)),
            pltpu.SemaphoreType.DMA((n_gy - 1,)),
            pltpu.SemaphoreType.DMA((n_gy - 1,)),
            pltpu.SemaphoreType.DMA((slots - 1,)),
            pltpu.SemaphoreType.DMA((slots - 1,)),
        ],
        compiler_params=pltpu.CompilerParams(
            collective_id=0, has_side_effects=True, vmem_limit_bytes=63 * 1024 * 1024
        ),
    )(
        vectors.reshape(K * STRIDE, COLS),
        background.reshape(V * L * ROWS, COLS),
        obs_site.reshape(groups, COLS),
        obs_offset,
        error,
    )
    analysis, obs = pl.pallas_call(
        mix_kernel,
        out_shape=(
            jax.ShapeDtypeStruct((K * STRIDE, COLS), f32),
            jax.ShapeDtypeStruct((K, obs_dev), f32),
        ),
        in_specs=[hbm] * 4,
        out_specs=(hbm, hbm),
        scratch_shapes=[
            pltpu.VMEM((L, V, ROWS, K, COLS), f32),
            pltpu.VMEM((groups, K, COLS), f32),
            pltpu.VMEM((K, COLS), f32),
            pltpu.VMEM((1, obs_dev), f32),
            pltpu.VMEM((K * STRIDE, COLS), f32),
            pltpu.VMEM((K, obs_dev), f32),
            pltpu.SemaphoreType.DMA((3 + V,)),
            pltpu.SemaphoreType.DMA((1 + V * K,)),
        ],
        compiler_params=pltpu.CompilerParams(vmem_limit_bytes=63 * 1024 * 1024),
    )(bred, proj, matrix, error)
    return analysis.reshape(vectors.shape), obs


def solution(mesh):
    placed = (
        P(None, None, None, "gx", "gy"),
        P(None, None, "gx", "gy"),
        P(("gx", "gy")),
        P(None, ("gx", "gy")),
        P(("gx", "gy")),
    )
    return jax.shard_map(
        functools.partial(local, mesh.shape["gx"], mesh.shape["gy"]),
        mesh=mesh,
        in_specs=placed,
        out_specs=(P(None, None, None, "gx", "gy"), P(None, ("gx", "gy"))),
        check_vma=False,
    )
```
